32 devices in a mesh: seq: 16 (over z, y, x), head: 2 (over core).
Axes of the slice: x: 2, y: 2, z: 4, core: 2. Of those that a mesh axis runs over, the one named last changes fastest.
Arguments:
- query_rows: bfloat16 [6144, 2048], P('seq', 'head'), may hold values from -41 to 41
- key_rows: bfloat16 [6144, 2048], P('seq', 'head'), may hold values from -4 to 4, as said below
- value_rows: bfloat16 [6144, 2048], P('seq', 'head'), may hold values from -6 to 6
- out_grad: bfloat16 [6144, 2048], P('seq'), may hold values from -6 to 6
- cluster_ids: int32 [16, 6144, 1], P('head', 'seq'), may hold values from 0 to 255; in each aligned block of 384 rows (0 to 383, 384 to 767, ..., all dimensions but the last counted through in order) at most 2 rows name the same one
- out_weight: bfloat16 [2048, 2048], P('head'), may hold values from -0.125 to 0.125
Outputs:
- layer_out: bfloat16 [6144, 2048], P('seq', 'head')
- query_grad: bfloat16 [6144, 2048], P('seq', 'head')
- key_grad: bfloat16 [6144, 2048], P('seq', 'head')
- value_grad: bfloat16 [6144, 2048], P('seq', 'head')
The draws below stay inside these ranges and needn't reach their ends.
Inputs may be any that keep to these rules, and one draw needn't show every extreme that they name: `cluster_ids`: in each head the 384 tokens of one index of seq (aligned blocks of the token dimension) name no cluster more than 2 times, a bound that some block reaches in every draw. `key_rows`: no token's key in any head is all zeros.
All inputs are finite; a program needn't handle non-finite values.
Results may differ from the reference program's by a relative error of at most 0.009.
Values may be sent and summed in bfloat16 or wider, within the bound.
A program may use at most 128 MiB of HBM per device.

```python
import math
import jax
import jax.numpy as jnp
import numpy as np
from jax import lax

HEADS = 16
DH = 128
D = 2048
CLUSTERS = 256
TOK_DEV = 384
MOST = 2
SLOTS = 32
TOKENS = 6144
N_SEQ = 16


def key_field(key):
    inner = jax.random.fold_in(key, 11)
    field = jnp.clip(jax.random.normal(inner, (TOKENS, HEADS * DH), jnp.float32), -4.0, 4.0)
    return field.astype(jnp.bfloat16).astype(jnp.float32)


def draw_key_rows(key, part):
    return key_field(key).astype(jnp.bfloat16)


def draw_query_rows(key, part):
    drawn = jnp.clip(jax.random.normal(jax.random.fold_in(key, 23), (TOKENS, HEADS * DH), jnp.float32), -4.0, 4.0)
    return drawn.astype(jnp.bfloat16)


def block_scale(stream_key, dims, cuts, low, largest):
    level = 1.0
    for position, parts in cuts:
        steps = jax.random.uniform(jax.random.fold_in(jax.random.fold_in(stream_key, 6), position), (parts,), jnp.float32, low / len(cuts), largest / len(cuts))
        level = level * jnp.repeat(jnp.exp(steps), dims[position] // parts).reshape((-1,) + (1,) * (len(dims) - 1 - position))
    return level


def routed_block(key, own, number, rows, number_of, top, most, skew):
    sequence = jax.random.permutation(key, number_of)
    packed, ordinary = shares(number_of, rows * top, most, skew, True), shares(number_of, rows * top, most, skew, False)
    places = jnp.arange(number_of)

    def named(sizes, offset_by):
        used = int((sizes > 0).sum())
        fixed = max(1, used // 4)
        passed = fixed + (places - fixed + offset_by * (used - fixed)) % max(1, number_of - fixed)
        return jnp.zeros((number_of,), jnp.int32).at[sequence[jnp.where(places < fixed, places, passed)]].set(jnp.asarray(sizes, jnp.int32))

    sizes = jnp.where(number % 4 == 0, named(packed, number // 4), named(ordinary, number - number // 4 - 1))
    mixed = jax.random.permutation(jax.random.fold_in(own, 3), number_of)
    source_of, sink = mixed[0:number_of // 2 * 2:2], mixed[1:number_of // 2 * 2:2]
    room = jnp.minimum(sizes[source_of] - 1, most - sizes[sink]) // 2
    room = jnp.where((source_of == sequence[0]) | (sink == sequence[0]) | (sizes[sink] == 0), 0, jnp.maximum(room, 0))
    passed = jax.random.randint(jax.random.fold_in(own, 4), (number_of // 2,), 0, 1 << 20) % (room + 1)
    sizes = sizes.at[source_of].add(-passed).at[sink].add(passed)
    labels = jnp.searchsorted(jnp.cumsum(sizes), jnp.arange(rows * top), side="right").astype(jnp.int32)
    table = labels.reshape(top, rows).T
    table = table[jax.random.permutation(jax.random.fold_in(own, 1), rows)]
    offset_by = jax.random.randint(jax.random.fold_in(own, 2), (rows, 1), 0, top)
    return jnp.take_along_axis(table, (jnp.arange(top)[None, :] + offset_by) % top, axis=1)


def shares(amount, total, reach, lean, full):
    loads = [(1 << 20) // math.isqrt(standing ** lean) + 1 for standing in range(1, amount + 1)]
    largest = reach if full else min(reach, max(-(-total // amount), total * loads[0] // sum(loads)))
    least = 1 if total - largest >= amount - 1 else 0
    counts, surplus = [largest] + [least] * (amount - 1), total - largest - least * (amount - 1)
    while surplus > 0:
        movable = [i for i in range(1, amount) if counts[i] < largest] or [i for i in range(1, amount) if counts[i] < reach]
        whole, budget = sum([loads[i] for i in movable]), surplus
        for i in movable:
            addition = min(reach - counts[i], max(1, budget * loads[i] // whole), surplus)
            counts[i] = counts[i] + addition
            surplus = surplus - addition
    return np.array(counts)


def noise(rng, dims, scale, most, cuts=(), held_as=jnp.bfloat16):
    gain = block_scale(rng, dims, cuts, -0.22, 0.18) if cuts else 1.0
    drawn = jax.random.normal(rng, dims, jnp.float32) * scale * gain
    return jnp.minimum(jnp.maximum(drawn, -most), most).astype(held_as)


def setup_inputs(seed: int = 0) -> dict:
    arg_keys = jax.random.split(jax.random.key(seed), 7)
    query_rows = draw_query_rows(jax.random.fold_in(arg_keys[6], 71), 0)
    key_rows = draw_key_rows(jax.random.fold_in(arg_keys[6], 71), 0)
    value_rows = noise(arg_keys[2], (TOKENS, HEADS * DH), 1.0, 6.0, ((0, 16), (1, 2)))
    out_grad = noise(arg_keys[3], (TOKENS, D), 1.0, 6.0, ((0, 16),))
    cluster_ids_keys = jax.random.split(jax.random.fold_in(arg_keys[4], 1), HEADS * TOKENS // TOK_DEV)
    cluster_ids_turns = jax.random.permutation(jax.random.fold_in(arg_keys[4], 3), HEADS * TOKENS // TOK_DEV)
    cluster_ids = jax.vmap(lambda own, number: routed_block(jax.random.fold_in(arg_keys[4], 2), own, number, TOK_DEV, CLUSTERS, 1, MOST, 2))(cluster_ids_keys, cluster_ids_turns).reshape((HEADS, TOKENS, 1))
    out_weight = noise(arg_keys[5], (HEADS * DH, D), (HEADS * DH) ** -0.5, 0.125, ((0, 2),))
    return dict(query_rows=query_rows, key_rows=key_rows, value_rows=value_rows, out_grad=out_grad, cluster_ids=cluster_ids, out_weight=out_weight)


NEGATIVE = -1.0e30


def slot_rows(cluster, per_cluster):
    count = cluster.shape[1]
    matches = cluster[:, :, None] == cluster[:, None, :]
    order_ids = jnp.arange(count, dtype=jnp.int32)
    earlier = order_ids[:, None] > order_ids[None, :]
    before = jnp.sum(jnp.logical_and(matches, earlier[None]).astype(jnp.int32), axis=2)
    return (cluster * per_cluster + before).astype(jnp.int32)


def cluster_attention(query_slots, key_slots, value_slots, grad_slots, occupied):
    scale = DH ** -0.5
    qf = query_slots.astype(jnp.float32)
    kf = key_slots.astype(jnp.float32)
    vf = value_slots.astype(jnp.float32)
    gf = grad_slots.astype(jnp.float32)
    scores = jnp.einsum("cqd,ckd->cqk", qf, kf) * scale
    order_ids = jnp.arange(query_slots.shape[1], dtype=jnp.int32)
    causal = order_ids[None, :] <= order_ids[:, None]
    allowed = jnp.logical_and(causal[None], occupied[:, None, :] > 0)
    scores = jnp.where(allowed, scores, NEGATIVE)
    row_max = jnp.max(scores, axis=2, keepdims=True)
    weights = jnp.exp(scores - row_max)
    probs_full = weights / jnp.sum(weights, axis=2, keepdims=True)
    probs_half = probs_full.astype(jnp.bfloat16)
    probs_back = probs_half.astype(jnp.float32)
    attn_out = jnp.einsum("cqk,ckd->cqd", probs_back, vf).astype(jnp.bfloat16)
    dprob = jnp.einsum("cqd,ckd->cqk", gf, vf)
    delta = jnp.sum(probs_full * dprob, axis=2, keepdims=True)
    dscore = (probs_full * (dprob - delta)).astype(jnp.bfloat16).astype(jnp.float32)
    query_grad = (jnp.einsum("cqk,ckd->cqd", dscore, kf) * scale).astype(jnp.bfloat16)
    key_grad = (jnp.einsum("cqk,cqd->ckd", dscore, qf) * scale).astype(jnp.bfloat16)
    value_grad = jnp.einsum("cqk,cqd->ckd", probs_back, gf).astype(jnp.bfloat16)
    return attn_out, query_grad, key_grad, value_grad


def reference(query_rows, key_rows, value_rows, out_grad, cluster_ids, out_weight):
    attn_grad = jnp.dot(out_grad, out_weight.T, preferred_element_type=jnp.float32).astype(jnp.bfloat16)

    def one_head(head_id):
        start = (head_id * DH).astype(jnp.int32)
        cluster = lax.dynamic_index_in_dim(cluster_ids, head_id, 0, keepdims=False)[:, 0]
        blocks = cluster.reshape(N_SEQ, TOK_DEV)
        source = jnp.arange(N_SEQ, dtype=jnp.int32)[:, None]
        slot_index = (slot_rows(blocks, SLOTS) + source * MOST).reshape(TOKENS).astype(jnp.int32)

        def to_slots(whole):
            rows = lax.dynamic_slice_in_dim(whole, start, DH, 1)
            table = jnp.zeros((CLUSTERS * SLOTS, DH), jnp.bfloat16).at[slot_index].set(rows)
            return table.reshape(CLUSTERS, SLOTS, DH)

        occupied = jnp.zeros((CLUSTERS * SLOTS,), jnp.bfloat16).at[slot_index].set(1.0).reshape(CLUSTERS, SLOTS)
        results = cluster_attention(to_slots(query_rows), to_slots(key_rows), to_slots(value_rows), to_slots(attn_grad), occupied)
        return tuple(item.reshape(CLUSTERS * SLOTS, DH)[slot_index] for item in results)

    attn_heads, query_heads, key_heads, value_heads = lax.map(one_head, jnp.arange(HEADS, dtype=jnp.int32))

    def to_tokens(stacked):
        return jnp.transpose(stacked, (1, 0, 2)).reshape(TOKENS, HEADS * DH)

    attn = to_tokens(attn_heads)
    layer_out = jnp.dot(attn, out_weight, preferred_element_type=jnp.float32).astype(jnp.bfloat16)
    return layer_out, to_tokens(query_heads), to_tokens(key_heads), to_tokens(value_heads)
```

```python
import functools

import jax
import jax.numpy as jnp
from jax import lax
from jax.experimental import pallas as pl
from jax.experimental.pallas import tpu as pltpu
from jax.sharding import PartitionSpec as P

CLUSTERS = 256
MOST = 2
QUARTERS = 4
LAG = 4
NEGATIVE = -1e30
MESH = pl.DeviceIdType.MESH
F32 = jnp.float32
BF16 = jnp.bfloat16


def dot(a, b, da, db):
    return lax.dot_general(a, b, (((da,), (db,)), ((), ())), preferred_element_type=F32)


def kernel(
    spots, heads, dh, nh,
    query, key, value, grad, ids_row, ids_col, weight,
    layer_out, query_grad, key_grad, value_grad,
    onehot, send, got, kv, zin, zup, zdown, back, total, half_out, half_in,
    as_, ar, kvs, kvr, zs, zr, bs, br, hs, hr,
):
    tokens = query.shape[0]
    slots = CLUSTERS * MOST
    rows = slots // spots
    step = 16
    tiles = rows // step
    quarter = spots * step
    two = 2 * dh
    four = 4 * dh
    scale = dh ** -0.5
    seq = lax.axis_index("seq")
    hd = lax.axis_index("head")
    z = seq // spots
    r = seq % spots

    def peer(k):
        return z * spots + (r + k) % spots

    barrier = pltpu.get_barrier_semaphore()
    for k in range(1, spots):
        pl.semaphore_signal(barrier, inc=1, device_id={"seq": peer(k)}, device_id_type=MESH)
    for k in range(1, nh):
        pl.semaphore_signal(barrier, inc=1, device_id={"head": (hd + k) % nh}, device_id_type=MESH)

    whole = QUARTERS * spots
    for to in ((seq + spots) % whole, (seq + whole - spots) % whole):
        pl.semaphore_signal(barrier, inc=1, device_id={"seq": to}, device_id_type=MESH)
    pl.semaphore_wait(barrier, spots - 1 + nh - 1 + 2)

    def remote(src, dst, ss, rs, to):
        return pltpu.make_async_remote_copy(
            src_ref=src, dst_ref=dst, send_sem=ss, recv_sem=rs,
            device_id={"seq": to}, device_id_type=MESH,
        )

    def out_copy(h, k):
        d = (r + k) % spots
        return remote(send.at[h, d], got.at[h, r], as_.at[h, k], ar.at[h, k], peer(k))

    def in_copy(h, k):
        s = (r + spots - k) % spots
        return remote(send.at[h, s], got.at[h, s], as_.at[h, k], ar.at[h, k], peer(k))

    def back_copy(h, k):
        d = (r + k) % spots
        return remote(send.at[h, d], back.at[h, r], bs.at[h, k], br.at[h, k], peer(k))

    def back_in(h, k):
        s = (r + spots - k) % spots
        return remote(send.at[h, s], back.at[h, s], bs.at[h, k], br.at[h, k], peer(k))

    low = pl.ds(0, two)
    high = pl.ds(two, two)
    above = jnp.minimum(seq + spots, QUARTERS * spots - 1)
    below = jnp.maximum(seq - spots, 0)

    def kv_first(h):
        return remote(got.at[h, :, :, low], kv.at[h, :, :, low], kvs.at[h, 1], kvr.at[h, 0], above)

    def kv_own(h):
        return remote(got.at[h, :, :, low], kv.at[h, :, :, high], kvs.at[h, 1], kvr.at[h, 1], above)

    def kv_forward(h):
        return remote(kv.at[h, :, :, low], kv.at[h, :, :, low], kvs.at[h, 0], kvr.at[h, 0], above)

    def top_down(h):
        return remote(got.at[h], zin.at[h], zs.at[h, 0], zr.at[h], below)

    def top_back(h):
        return remote(zup.at[h], zin.at[h], zs.at[h, 0], zr.at[h], above)

    def sums_down(h):
        return remote(zdown.at[h], zin.at[h], zs.at[h, 1], zr.at[h], below)

    def last_down(h):
        return remote(zdown.at[h, :, :, low], zin.at[h, :, :, low], zs.at[h, 1], zr.at[h], below)

    def columns(h):
        return pl.ds(pl.multiple_of(h * dh, dh), dh)

    def fill(h, carry):
        cols = columns(h)
        row = ids_row[h]
        col = ids_col[h]
        at0 = lax.broadcasted_iota(jnp.int32, (tokens, tokens), 0)
        at1 = lax.broadcasted_iota(jnp.int32, (tokens, tokens), 1)
        same = jnp.logical_and(col == row, at0 < at1)
        before = jnp.sum(jnp.where(same, 1, 0), axis=0, keepdims=True)
        slot = row * MOST + before
        place = lax.broadcasted_iota(jnp.int32, (slots, tokens), 0)
        picked = jnp.where(place == slot, 1.0, 0.0).astype(BF16)
        onehot[h] = picked
        attn_grad = dot(grad[...], weight[cols, :], 1, 1).astype(BF16)
        for c, x in enumerate((key[:, cols], value[:, cols], query[:, cols], attn_grad)):
            send[h, :, :, c * dh:(c + 1) * dh] = dot(picked, x, 1, 0).astype(BF16).reshape(spots, rows, dh)
        for k in range(1, spots):
            out_copy(h, k).start()
        got[h, r] = send[h, r]
        return carry

    lax.fori_loop(0, heads, fill, 0)
    total[...] = jnp.zeros_like(total)

    chunk = min(spots, 4)
    chunks = spots // chunk

    def attend(h, g, nk, both):
        at = pl.ds(pl.multiple_of(g * step, step), step)
        flat = lambda x: x.reshape(x.shape[0] * step, x.shape[2])
        own = flat(got[h, :, at, low])
        if both:
            parts = [flat(kv[h, :, at, low]), flat(kv[h, :, at, high]), own, flat(zin[h, :, at, low])]
        elif nk == 2:
            parts = [flat(kv[h, :, at, low]), own]
        else:
            parts = [own]
        kvs_all = jnp.concatenate(parts, axis=0) if nk > 1 else own
        keys, values = kvs_all[:, :dh], kvs_all[:, dh:]
        nkeys = nk * quarter
        nq = chunk * step * (2 if both else 1)
        j = lax.broadcasted_iota(jnp.int32, (nkeys, 1), 0)
        occupied = jnp.max(jnp.abs(keys.astype(F32)), axis=1, keepdims=True) > 0
        cluster_k = jnp.where(occupied, (j & 15) >> 1, -1)
        rank_k = (j >> 4) * 2 + (j & 1)
        i = lax.broadcasted_iota(jnp.int32, (1, nq), 1)
        cluster_q = (i & 15) >> 1
        own_at = nk - (2 if both else 1)

        def part(c):
            if chunks == 1:
                mine = slice(None)
            else:
                mine = pl.ds(c * chunk, chunk)
            qg = flat(got[h, mine, at, high])
            if both:
                qg = jnp.concatenate([qg, flat(zin[h, mine, at, high])], axis=0)
            q, dout = qg[:, :dh], qg[:, dh:]
            if both:
                second = (i >= chunk * step).astype(jnp.int32)
            else:
                second = 0
            src = c * chunk + ((i - second * (chunk * step)) >> 4)
            rank_q = ((own_at + second) * spots + src) * 2 + (i & 1)
            allowed = jnp.logical_and(cluster_k == cluster_q, rank_k <= rank_q)
            scores = jnp.where(allowed, dot(keys, q, 1, 1) * scale, NEGATIVE)
            w = jnp.exp(scores - jnp.max(scores, axis=0, keepdims=True))
            probs = w * (1.0 / jnp.sum(w, axis=0, keepdims=True))
            probs_half = probs.astype(BF16)
            dprob = dot(values, dout, 1, 1)
            delta = jnp.sum(probs * dprob, axis=0, keepdims=True)
            dscore = (probs * (dprob - delta)).astype(BF16)
            dq = (dot(dscore, keys, 0, 0) * scale).astype(BF16)
            attn = dot(probs_half, values, 0, 0).astype(BF16)
            half = chunk * step
            for x, c0 in ((dq, two), (attn, two + dh)):
                send[h, mine, at, c0:c0 + dh] = x[:half].reshape(chunk, step, dh)
                if both:
                    zup[h, mine, at, c0:c0 + dh] = x[half:].reshape(chunk, step, dh)
            return dot(dscore, q, 1, 0) * scale, dot(probs_half, dout, 1, 0)

        if chunks == 1:
            dk, dv = part(0)
        else:
            def more(c, sums):
                a, b = part(c)
                return sums[0] + a, sums[1] + b
            zero = jnp.zeros((nkeys, dh), F32)
            dk, dv = lax.fori_loop(0, chunks, more, (zero, zero))
        for x, c0 in ((dk.astype(BF16), 0), (dv.astype(BF16), dh)):
            cut = lambda a: x[a * quarter:(a + 1) * quarter].reshape(spots, step, dh)
            send[h, :, at, c0:c0 + dh] = cut(own_at)
            if nk > 1:
                zdown[h, :, at, c0:c0 + dh] = cut(0)
            if both:
                zdown[h, :, at, two + c0:two + c0 + dh] = cut(1)
                zup[h, :, at, c0:c0 + dh] = cut(3)

    def attend_all(h, nk, both):
        def one(g, carry):
            attend(h, g, nk, both)
            return carry
        lax.fori_loop(0, tiles, one, 0)

    def push(h):
        for k in range(1, spots):
            in_copy(h, k).wait_recv()
        for k in range(1, spots):
            out_copy(h, k).wait_send()

        @pl.when(z == 0)
        def _():
            kv_first(h).start()
            attend_all(h, 1, False)

        @pl.when(z == 1)
        def _():
            kv_own(h).start()
            kv_forward(h).wait_recv()
            kv_forward(h).start()
            attend_all(h, 2, False)

        @pl.when(z == 2)
        def _():
            kv_forward(h).wait_recv()
            kv_own(h).wait_recv()
            top_down(h).wait_recv()
            attend_all(h, 4, True)
            sums_down(h).start()
            top_back(h).start()

        @pl.when(z == 3)
        def _():
            top_down(h).start()

    def give_back(h):
        @pl.when(z == 0)
        def _():
            last_down(h).wait_recv()
            send[h, :, :, low] = (send[h, :, :, low].astype(F32) + zin[h, :, :, low].astype(F32)).astype(BF16)

        @pl.when(z == 1)
        def _():
            sums_down(h).wait_recv()
            zdown[h, :, :, low] = (zdown[h, :, :, low].astype(F32) + zin[h, :, :, low].astype(F32)).astype(BF16)
            last_down(h).start()
            send[h, :, :, low] = (send[h, :, :, low].astype(F32) + zin[h, :, :, high].astype(F32)).astype(BF16)

        @pl.when(z == 3)
        def _():
            top_back(h).wait_recv()
            send[h] = zin[h]

        for k in range(1, spots):
            back_copy(h, k).start()
        back[h, r] = send[h, r]

    def finish(h):
        cols = columns(h)
        for k in range(1, spots):
            back_in(h, k).wait_recv()
        picked = onehot[h]
        for c, out in ((0, key_grad), (1, value_grad), (2, query_grad)):
            block = back[h, :, :, c * dh:(c + 1) * dh].reshape(slots, dh)
            out[:, cols] = dot(picked, block, 0, 0).astype(BF16)
        attn = dot(picked, back[h, :, :, 3 * dh:four].reshape(slots, dh), 0, 0).astype(BF16)
        total[...] += dot(attn, weight[cols, :], 1, 0)

    def turn(i, carry):
        @pl.when(i < heads)
        def _():
            push(i)

        @pl.when(i >= LAG + 1)
        def _():
            finish(i - LAG - 1)

        @pl.when(jnp.logical_and(i >= LAG, i < heads + LAG))
        def _():
            give_back(i - LAG)

        return carry

    lax.fori_loop(0, heads + LAG + 1, turn, 0)

    width = layer_out.shape[1]

    def share(k):
        return pltpu.make_async_remote_copy(
            src_ref=half_out.at[k - 1], dst_ref=half_in.at[k - 1],
            send_sem=hs.at[k - 1], recv_sem=hr.at[k - 1],
            device_id={"head": (hd + k) % nh}, device_id_type=MESH,
        )

    for k in range(1, nh):
        to = (hd + k) % nh
        half_out[k - 1] = total[:, pl.ds(pl.multiple_of(to * width, width), width)].astype(BF16)
        share(k).start()
    mine = total[:, pl.ds(pl.multiple_of(hd * width, width), width)]

    def settle(h, carry):
        for k in range(1, spots):
            back_copy(h, k).wait_send()

        @pl.when(z == 0)
        def _():
            kv_first(h).wait_send()

        @pl.when(z == 1)
        def _():
            kv_own(h).wait_send()
            kv_forward(h).wait_send()
            last_down(h).wait_send()

        @pl.when(z == 2)
        def _():
            sums_down(h).wait_send()
            top_back(h).wait_send()

        @pl.when(z == 3)
        def _():
            top_down(h).wait_send()

        return carry

    lax.fori_loop(0, heads, settle, 0)
    for k in range(1, nh):
        share(k).wait()
        mine = mine + half_in[k - 1].astype(F32)
    layer_out[...] = mine.astype(BF16)


def body(nseq, nh, query_rows, key_rows, value_rows, out_grad, cluster_ids, out_weight):
    tokens, wide = query_rows.shape
    heads = cluster_ids.shape[0]
    dh = wide // heads
    spots = nseq // QUARTERS
    rows = CLUSTERS * MOST // spots
    model = out_weight.shape[1]
    out = jax.ShapeDtypeStruct((tokens, wide), BF16)
    vm = pl.BlockSpec(memory_space=pltpu.VMEM)
    full = pltpu.VMEM((heads, spots, rows, 4 * dh), BF16)
    dma = pltpu.SemaphoreType.DMA
    width = model // nh
    return pl.pallas_call(
        functools.partial(kernel, spots, heads, dh, nh),
        out_shape=(jax.ShapeDtypeStruct((tokens, width), BF16), out, out, out),
        in_specs=[vm] * 7,
        out_specs=(vm,) * 4,
        scratch_shapes=[
            pltpu.VMEM((heads, CLUSTERS * MOST, tokens), BF16),
            full, full, full, full, full, full, full,
            pltpu.VMEM((tokens, model), F32),
            pltpu.VMEM((nh - 1, tokens, width), BF16),
            pltpu.VMEM((nh - 1, tokens, width), BF16),
            dma((heads, spots)), dma((heads, spots)),
            dma((heads, 2)), dma((heads, 2)),
            dma((heads, 2)), dma((heads,)),
            dma((heads, spots)), dma((heads, spots)),
            dma((nh - 1,)), dma((nh - 1,)),
        ],
        compiler_params=pltpu.CompilerParams(
            collective_id=0, has_side_effects=True, vmem_limit_bytes=60 * 2**20
        ),
        cost_estimate=pl.CostEstimate(flops=10**10, bytes_accessed=2**24, transcendentals=2**21),
    )(
        query_rows, key_rows, value_rows, out_grad,
        cluster_ids.reshape(heads, 1, tokens), cluster_ids, out_weight,
    )


def solution(mesh):
    in_specs = (
        P("seq", "head"),
        P("seq", "head"),
        P("seq", "head"),
        P("seq", None),
        P("head", "seq", None),
        P("head", None),
    )
    out_specs = (P("seq", "head"), P("seq", "head"), P("seq", "head"), P("seq", "head"))
    run = functools.partial(body, mesh.shape["seq"], mesh.shape["head"])
    return jax.shard_map(run, mesh=mesh, in_specs=in_specs, out_specs=out_specs, check_vma=False)
```

```python
import functools

import jax
import jax.numpy as jnp
from jax import lax
from jax.experimental import pallas as pl
from jax.experimental.pallas import tpu as pltpu
from jax.sharding import PartitionSpec as P

CLUSTERS = 256
MOST = 2
QUARTERS = 4
LAG = 6
NEGATIVE = -1e30
MESH = pl.DeviceIdType.MESH
F32 = jnp.float32
BF16 = jnp.bfloat16


def dot(a, b, da, db):
    return lax.dot_general(a, b, (((da,), (db,)), ((), ())), preferred_element_type=F32)


def kernel(
    spots, heads, split, dh, nh,
    query, key, value, grad, ids_row, weight,
    layer_out, query_grad, key_grad, value_grad,
    onehot, earlier, attn_all, send, got, kv, zin, zup, zdown, back, total, half_out, half_in,
    as_, ar, kvs, kvr, zs, zr, bs, br, hs, hr,
):
    tokens = query.shape[0]
    slots = CLUSTERS * MOST
    rows = slots // spots // split
    units = heads * split
    step = 16
    tiles = rows // step
    quarter = spots * step
    two = 2 * dh
    four = 4 * dh
    scale = dh ** -0.5
    seq = lax.axis_index("seq")
    hd = lax.axis_index("head")
    z = seq // spots
    r = seq % spots

    def peer(k):
        return z * spots + (r + k) % spots

    barrier = pltpu.get_barrier_semaphore()
    for k in range(1, spots):
        pl.semaphore_signal(barrier, inc=1, device_id={"seq": peer(k)}, device_id_type=MESH)
    for k in range(1, nh):
        pl.semaphore_signal(barrier, inc=1, device_id={"head": (hd + k) % nh}, device_id_type=MESH)

    whole = QUARTERS * spots
    for to in ((seq + spots) % whole, (seq + whole - spots) % whole):
        pl.semaphore_signal(barrier, inc=1, device_id={"seq": to}, device_id_type=MESH)
    pl.semaphore_wait(barrier, spots - 1 + nh - 1 + 2)

    def remote(src, dst, ss, rs, to):
        return pltpu.make_async_remote_copy(
            src_ref=src, dst_ref=dst, send_sem=ss, recv_sem=rs,
            device_id={"seq": to}, device_id_type=MESH,
        )

    def out_copy(h, k):
        d = (r + k) % spots
        return remote(send.at[h, d], got.at[h, r], as_.at[h, k], ar.at[h, k], peer(k))

    def in_copy(h, k):
        s = (r + spots - k) % spots
        return remote(send.at[h, s], got.at[h, s], as_.at[h, k], ar.at[h, k], peer(k))

    def back_copy(h, k):
        d = (r + k) % spots
        return remote(send.at[h, d], back.at[h, r], bs.at[h, k], br.at[h, k], peer(k))

    def back_in(h, k):
        s = (r + spots - k) % spots
        return remote(send.at[h, s], back.at[h, s], bs.at[h, k], br.at[h, k], peer(k))

    low = pl.ds(0, two)
    high = pl.ds(two, two)
    above = jnp.minimum(seq + spots, QUARTERS * spots - 1)
    below = jnp.maximum(seq - spots, 0)

    def kv_first(h):
        return remote(got.at[h, :, :, low], kv.at[h, :, :, low], kvs.at[h, 1], kvr.at[h, 0], above)

    def kv_own(h):
        return remote(got.at[h, :, :, low], kv.at[h, :, :, high], kvs.at[h, 1], kvr.at[h, 1], above)

    def kv_forward(h):
        return remote(kv.at[h, :, :, low], kv.at[h, :, :, low], kvs.at[h, 0], kvr.at[h, 0], above)

    def top_down(h):
        return remote(got.at[h], zin.at[h], zs.at[h, 0], zr.at[h], below)

    def top_back(h):
        return remote(zup.at[h], zin.at[h], zs.at[h, 0], zr.at[h], above)

    def sums_down(h):
        return remote(zdown.at[h], zin.at[h], zs.at[h, 1], zr.at[h], below)

    def last_down(h):
        return remote(zdown.at[h, :, :, low], zin.at[h, :, :, low], zs.at[h, 1], zr.at[h], below)

    def columns(h):
        return pl.ds(pl.multiple_of(h * dh, dh), dh)

    at0 = lax.broadcasted_iota(jnp.int32, (tokens, tokens), 0)
    at1 = lax.broadcasted_iota(jnp.int32, (tokens, tokens), 1)
    earlier[...] = jnp.where(at0 < at1, 1.0, 0.0).astype(BF16)

    def fill(h, carry):
        cols = columns(h)
        row = ids_row[h]
        named = lax.broadcasted_iota(jnp.int32, (CLUSTERS, tokens), 0) == row
        counts = dot(jnp.where(named, 1.0, 0.0).astype(BF16), earlier[...], 1, 0)
        before = jnp.sum(jnp.where(named, counts, 0.0), axis=0, keepdims=True).astype(jnp.int32)
        slot = row * MOST + before
        place = lax.broadcasted_iota(jnp.int32, (slots, tokens), 0)
        picked = jnp.where(place == slot, 1.0, 0.0).astype(BF16)
        onehot[h] = picked
        attn_grad = dot(grad[...], weight[cols, :], 1, 1).astype(BF16)
        wide = jnp.concatenate([key[:, cols], value[:, cols], query[:, cols], attn_grad], axis=1)
        table = dot(picked, wide, 1, 0).astype(BF16).reshape(spots, split, rows, four)
        for part in range(split):
            u = h * split + part
            send[u] = table[:, part]
            for k in range(1, spots):
                out_copy(u, k).start()
            got[u, r] = send[u, r]
        return carry

    lax.fori_loop(0, heads, fill, 0)
    total[...] = jnp.zeros_like(total)

    chunk = min(spots, 4)
    chunks = spots // chunk

    def flat(x):
        return x.reshape(x.shape[0] * step, x.shape[2])

    def attend(h, g, nk, both):
        at = pl.ds(pl.multiple_of(g * step, step), step)
        own = flat(got[h, :, at, low])
        if both:
            parts = [flat(kv[h, :, at, low]), flat(kv[h, :, at, high]), own, flat(zin[h, :, at, low])]
        elif nk == 2:
            parts = [flat(kv[h, :, at, low]), own]
        else:
            parts = [own]
        kvs_all = jnp.concatenate(parts, axis=0) if nk > 1 else own
        keys, values = kvs_all[:, :dh], kvs_all[:, dh:]
        nkeys = nk * quarter
        half = chunk * step
        nq = half * (2 if both else 1)
        j = lax.broadcasted_iota(jnp.int32, (nkeys, 1), 0)
        occupied = jnp.max(jnp.abs(keys.astype(F32)), axis=1, keepdims=True) > 0
        cluster_k = jnp.where(occupied, (j & 15) >> 1, -1)
        rank_k = (j >> 4) * 2 + (j & 1)
        i = lax.broadcasted_iota(jnp.int32, (1, nq), 1)
        cluster_q = (i & 15) >> 1
        own_at = nk - (2 if both else 1)
        dk = dv = None
        for c in range(chunks):
            mine = pl.ds(c * chunk, chunk)
            qg = flat(got[h, mine, at, high])
            if both:
                qg = jnp.concatenate([qg, flat(zin[h, mine, at, high])], axis=0)
            q, dout = qg[:, :dh], qg[:, dh:]
            yield
            raw = dot(keys, q, 1, 1)
            dprob = dot(values, dout, 1, 1)
            yield
            second = (i >= half).astype(jnp.int32) if both else 0
            src = c * chunk + ((i - second * half) >> 4)
            rank_q = ((own_at + second) * spots + src) * 2 + (i & 1)
            allowed = jnp.logical_and(cluster_k == cluster_q, rank_k <= rank_q)
            scores = jnp.where(allowed, raw * scale, NEGATIVE)
            w = jnp.exp(scores - jnp.max(scores, axis=0, keepdims=True))
            probs = w * (1.0 / jnp.sum(w, axis=0, keepdims=True))
            probs_half = probs.astype(BF16)
            delta = jnp.sum(probs * dprob, axis=0, keepdims=True)
            dscore = (probs * (dprob - delta)).astype(BF16)
            yield
            dq = (dot(dscore, keys, 0, 0) * scale).astype(BF16)
            attn = dot(probs_half, values, 0, 0).astype(BF16)
            more_k = dot(dscore, q, 1, 0)
            more_v = dot(probs_half, dout, 1, 0)
            dk = more_k if dk is None else dk + more_k
            dv = more_v if dv is None else dv + more_v
            yield
            for x, c0 in ((dq, two), (attn, two + dh)):
                send[h, mine, at, c0:c0 + dh] = x[:half].reshape(chunk, step, dh)
                if both:
                    zup[h, mine, at, c0:c0 + dh] = x[half:].reshape(chunk, step, dh)
        for x, c0 in (((dk * scale).astype(BF16), 0), (dv.astype(BF16), dh)):
            def cut(a):
                return x[a * quarter:(a + 1) * quarter].reshape(spots, step, dh)
            send[h, :, at, c0:c0 + dh] = cut(own_at)
            if nk > 1:
                zdown[h, :, at, c0:c0 + dh] = cut(0)
            if both:
                zdown[h, :, at, two + c0:two + c0 + dh] = cut(1)
                zup[h, :, at, c0:c0 + dh] = cut(3)

    together = 2 if tiles % 2 == 0 else 1

    def attend_all(h, nk, both):
        def some(g, carry):
            work = [attend(h, g * together + t, nk, both) for t in range(together)]
            while work:
                work = [w for w in work if next(w, True) is None]
            return carry
        lax.fori_loop(0, tiles // together, some, 0)

    def return_rows(h):
        for k in range(1, spots):
            back_copy(h, k).start()
        back[h, r] = send[h, r]

    def push(h):
        for k in range(1, spots):
            in_copy(h, k).wait_recv()
        for k in range(1, spots):
            out_copy(h, k).wait_send()

        @pl.when(z == 0)
        def _():
            kv_first(h).start()
            attend_all(h, 1, False)

        @pl.when(z == 1)
        def _():
            kv_own(h).start()
            kv_forward(h).wait_recv()
            kv_forward(h).start()
            attend_all(h, 2, False)

        @pl.when(z == 2)
        def _():
            kv_forward(h).wait_recv()
            kv_own(h).wait_recv()
            top_down(h).wait_recv()
            attend_all(h, 4, True)
            sums_down(h).start()
            top_back(h).start()
            return_rows(h)

        @pl.when(z == 3)
        def _():
            top_down(h).start()

    def give_back(h):
        @pl.when(z == 0)
        def _():
            last_down(h).wait_recv()
            send[h, :, :, low] = (send[h, :, :, low].astype(F32) + zin[h, :, :, low].astype(F32)).astype(BF16)

        @pl.when(z == 1)
        def _():
            sums_down(h).wait_recv()
            zdown[h, :, :, low] = (zdown[h, :, :, low].astype(F32) + zin[h, :, :, low].astype(F32)).astype(BF16)
            last_down(h).start()
            send[h, :, :, low] = (send[h, :, :, low].astype(F32) + zin[h, :, :, high].astype(F32)).astype(BF16)

        @pl.when(z == 3)
        def _():
            top_back(h).wait_recv()
            send[h] = zin[h]

        @pl.when(z != 2)
        def _():
            return_rows(h)

    def finish(h):
        cols = columns(h)
        for part in range(split):
            for k in range(1, spots):
                back_in(h * split + part, k).wait_recv()
        table = jnp.stack([back[h * split + part] for part in range(split)], axis=1).reshape(slots, four)
        rows_back = dot(onehot[h], table, 0, 0).astype(BF16)
        key_grad[:, cols] = rows_back[:, :dh]
        value_grad[:, cols] = rows_back[:, dh:two]
        query_grad[:, cols] = rows_back[:, two:two + dh]
        attn_all[:, cols] = rows_back[:, two + dh:]

        @pl.when(h % pair == pair - 1)
        def _():
            both = pl.ds(pl.multiple_of((h - (pair - 1)) * dh, pair * dh), pair * dh)
            total[...] += dot(attn_all[:, both], weight[both, :], 1, 0)

    pair = 2 if heads % 2 == 0 else 1

    def turn(i, carry):
        @pl.when(i < units)
        def _():
            push(i)

        @pl.when(jnp.logical_and(i >= LAG + 1, (i - LAG - 1) % split == split - 1))
        def _():
            finish((i - LAG - 1) // split)

        @pl.when(jnp.logical_and(i >= LAG, i < units + LAG))
        def _():
            give_back(i - LAG)

        return carry

    lax.fori_loop(0, units + LAG + 1, turn, 0)

    width = layer_out.shape[1]

    def share(k):
        return pltpu.make_async_remote_copy(
            src_ref=half_out.at[k - 1], dst_ref=half_in.at[k - 1],
            send_sem=hs.at[k - 1], recv_sem=hr.at[k - 1],
            device_id={"head": (hd + k) % nh}, device_id_type=MESH,
        )

    for k in range(1, nh):
        to = (hd + k) % nh
        half_out[k - 1] = total[:, pl.ds(pl.multiple_of(to * width, width), width)].astype(BF16)
        share(k).start()
    mine = total[:, pl.ds(pl.multiple_of(hd * width, width), width)]

    def settle(h, carry):
        for k in range(1, spots):
            back_copy(h, k).wait_send()

        @pl.when(z == 0)
        def _():
            kv_first(h).wait_send()

        @pl.when(z == 1)
        def _():
            kv_own(h).wait_send()
            kv_forward(h).wait_send()
            last_down(h).wait_send()

        @pl.when(z == 2)
        def _():
            sums_down(h).wait_send()
            top_back(h).wait_send()

        @pl.when(z == 3)
        def _():
            top_down(h).wait_send()

        return carry

    lax.fori_loop(0, units, settle, 0)
    for k in range(1, nh):
        share(k).wait()
        mine = mine + half_in[k - 1].astype(F32)
    layer_out[...] = mine.astype(BF16)


def body(nseq, nh, query_rows, key_rows, value_rows, out_grad, cluster_ids, out_weight):
    tokens, wide = query_rows.shape
    heads = cluster_ids.shape[0]
    dh = wide // heads
    spots = nseq // QUARTERS
    rows = CLUSTERS * MOST // spots
    split = 2 if rows % 32 == 0 else 1
    units = heads * split
    model = out_weight.shape[1]
    out = jax.ShapeDtypeStruct((tokens, wide), BF16)
    vm = pl.BlockSpec(memory_space=pltpu.VMEM)
    full = pltpu.VMEM((units, spots, rows // split, 4 * dh), BF16)
    dma = pltpu.SemaphoreType.DMA
    width = model // nh
    return pl.pallas_call(
        functools.partial(kernel, spots, heads, split, dh, nh),
        out_shape=(jax.ShapeDtypeStruct((tokens, width), BF16), out, out, out),
        in_specs=[vm] * 6,
        out_specs=(vm,) * 4,
        scratch_shapes=[
            pltpu.VMEM((heads, CLUSTERS * MOST, tokens), BF16),
            pltpu.VMEM((tokens, tokens), BF16),
            pltpu.VMEM((tokens, wide), BF16),
            full, full, full, full, full, full, full,
            pltpu.VMEM((tokens, model), F32),
            pltpu.VMEM((nh - 1, tokens, width), BF16),
            pltpu.VMEM((nh - 1, tokens, width), BF16),
            dma((units, spots)), dma((units, spots)),
            dma((units, 2)), dma((units, 2)),
            dma((units, 2)), dma((units,)),
            dma((units, spots)), dma((units, spots)),
            dma((nh - 1,)), dma((nh - 1,)),
        ],
        compiler_params=pltpu.CompilerParams(
            collective_id=0, has_side_effects=True, vmem_limit_bytes=60 * 2**20
        ),
        cost_estimate=pl.CostEstimate(flops=10**10, bytes_accessed=2**24, transcendentals=2**21),
    )(
        query_rows, key_rows, value_rows, out_grad,
        cluster_ids.reshape(heads, 1, tokens), out_weight,
    )


def solution(mesh):
    in_specs = (
        P("seq", "head"),
        P("seq", "head"),
        P("seq", "head"),
        P("seq", None),
        P("head", "seq", None),
        P("head", None),
    )
    out_specs = (P("seq", "head"), P("seq", "head"), P("seq", "head"), P("seq", "head"))
    run = functools.partial(body, mesh.shape["seq"], mesh.shape["head"])
    return jax.shard_map(run, mesh=mesh, in_specs=in_specs, out_specs=out_specs, check_vma=False)
```

```python
import functools

import jax
import jax.numpy as jnp
from jax import lax
from jax.experimental import pallas as pl
from jax.experimental.pallas import tpu as pltpu
from jax.sharding import PartitionSpec as P

CLUSTERS = 256
MOST = 2
QUARTERS = 4
LAG = 6
AHEAD = 3
NEGATIVE = -1e30
MESH = pl.DeviceIdType.MESH
F32 = jnp.float32
BF16 = jnp.bfloat16


def dot(a, b, da, db):
    return lax.dot_general(a, b, (((da,), (db,)), ((), ())), preferred_element_type=F32)


def kernel(
    spots, heads, split, dh, nh,
    query, key, value, grad, ids_row, weight,
    layer_out, query_grad, key_grad, value_grad,
    onehot, earlier, attn_all, send, got, kv, zin, zup, zdown, back, total, half_out, half_in,
    as_, ar, kvs, kvr, zs, zr, bs, br, hs, hr,
):
    tokens = query.shape[0]
    slots = CLUSTERS * MOST
    rows = slots // spots // split
    units = heads * split
    step = 16
    tiles = rows // step
    quarter = spots * step
    two = 2 * dh
    four = 4 * dh
    scale = dh ** -0.5
    seq = lax.axis_index("seq")
    hd = lax.axis_index("head")
    z = seq // spots
    r = seq % spots

    def peer(k):
        return z * spots + (r + k) % spots

    barrier = pltpu.get_barrier_semaphore()
    for k in range(1, spots):
        pl.semaphore_signal(barrier, inc=1, device_id={"seq": peer(k)}, device_id_type=MESH)
    for k in range(1, nh):
        pl.semaphore_signal(barrier, inc=1, device_id={"head": (hd + k) % nh}, device_id_type=MESH)

    whole = QUARTERS * spots
    for to in ((seq + spots) % whole, (seq + whole - spots) % whole):
        pl.semaphore_signal(barrier, inc=1, device_id={"seq": to}, device_id_type=MESH)
    pl.semaphore_wait(barrier, spots - 1 + nh - 1 + 2)

    def remote(src, dst, ss, rs, to):
        return pltpu.make_async_remote_copy(
            src_ref=src, dst_ref=dst, send_sem=ss, recv_sem=rs,
            device_id={"seq": to}, device_id_type=MESH,
        )

    def out_copy(h, k):
        d = (r + k) % spots
        return remote(send.at[h, d], got.at[h, r], as_.at[h, k], ar.at[h, k], peer(k))

    def in_copy(h, k):
        s = (r + spots - k) % spots
        return remote(send.at[h, s], got.at[h, s], as_.at[h, k], ar.at[h, k], peer(k))

    def back_copy(h, k):
        d = (r + k) % spots
        return remote(send.at[h, d], back.at[h, r], bs.at[h, k], br.at[h, k], peer(k))

    def back_in(h, k):
        s = (r + spots - k) % spots
        return remote(send.at[h, s], back.at[h, s], bs.at[h, k], br.at[h, k], peer(k))

    low = pl.ds(0, two)
    high = pl.ds(two, two)
    above = jnp.minimum(seq + spots, QUARTERS * spots - 1)
    below = jnp.maximum(seq - spots, 0)

    def kv_first(h):
        return remote(got.at[h, :, :, low], kv.at[h, :, :, low], kvs.at[h, 1], kvr.at[h, 0], above)

    def kv_own(h):
        return remote(got.at[h, :, :, low], kv.at[h, :, :, high], kvs.at[h, 1], kvr.at[h, 1], above)

    def kv_forward(h):
        return remote(kv.at[h, :, :, low], kv.at[h, :, :, low], kvs.at[h, 0], kvr.at[h, 0], above)

    def top_down(h):
        return remote(got.at[h], zin.at[h], zs.at[h, 0], zr.at[h], below)

    def top_back(h):
        return remote(zup.at[h], zin.at[h], zs.at[h, 0], zr.at[h], above)

    def sums_down(h):
        return remote(zdown.at[h], zin.at[h], zs.at[h, 1], zr.at[h], below)

    def last_down(h):
        return remote(zdown.at[h, :, :, low], zin.at[h, :, :, low], zs.at[h, 1], zr.at[h], below)

    def columns(h):
        return pl.ds(pl.multiple_of(h * dh, dh), dh)

    at0 = lax.broadcasted_iota(jnp.int32, (tokens, tokens), 0)
    at1 = lax.broadcasted_iota(jnp.int32, (tokens, tokens), 1)
    earlier[...] = jnp.where(at0 < at1, 1.0, 0.0).astype(BF16)

    def fill(h):
        cols = columns(h)
        row = ids_row[h]
        named = lax.broadcasted_iota(jnp.int32, (CLUSTERS, tokens), 0) == row
        counts = dot(jnp.where(named, 1.0, 0.0).astype(BF16), earlier[...], 1, 0)
        before = jnp.sum(jnp.where(named, counts, 0.0), axis=0, keepdims=True).astype(jnp.int32)
        slot = row * MOST + before
        place = lax.broadcasted_iota(jnp.int32, (slots, tokens), 0)
        picked = jnp.where(place == slot, 1.0, 0.0).astype(BF16)
        onehot[h] = picked
        attn_grad = dot(grad[...], weight[cols, :], 1, 1).astype(BF16)
        wide = jnp.concatenate([key[:, cols], value[:, cols], query[:, cols], attn_grad], axis=1)
        table = dot(picked, wide, 1, 0).astype(BF16).reshape(spots, split, rows, four)
        for part in range(split):
            u = h * split + part
            send[u] = table[:, part]
            for k in range(1, spots):
                out_copy(u, k).start()
            got[u, r] = send[u, r]

    total[...] = jnp.zeros_like(total)

    chunk = min(spots, 4)
    chunks = spots // chunk

    def flat(x):
        return x.reshape(x.shape[0] * step, x.shape[2])

    def attend(h, g, nk, both):
        at = pl.ds(pl.multiple_of(g * step, step), step)
        own = flat(got[h, :, at, low])
        if both:
            parts = [flat(kv[h, :, at, low]), flat(kv[h, :, at, high]), own, flat(zin[h, :, at, low])]
        elif nk == 2:
            parts = [flat(kv[h, :, at, low]), own]
        else:
            parts = [own]
        kvs_all = jnp.concatenate(parts, axis=0) if nk > 1 else own
        keys, values = kvs_all[:, :dh], kvs_all[:, dh:]
        nkeys = nk * quarter
        half = chunk * step
        nq = half * (2 if both else 1)
        j = lax.broadcasted_iota(jnp.int32, (nkeys, 1), 0)
        occupied = jnp.max(jnp.abs(keys.astype(F32)), axis=1, keepdims=True) > 0
        cluster_k = jnp.where(occupied, (j & 15) >> 1, -1)
        rank_k = (j >> 4) * 2 + (j & 1)
        i = lax.broadcasted_iota(jnp.int32, (1, nq), 1)
        cluster_q = (i & 15) >> 1
        own_at = nk - (2 if both else 1)
        dk = dv = None
        for c in range(chunks):
            mine = pl.ds(c * chunk, chunk)
            qg = flat(got[h, mine, at, high])
            if both:
                qg = jnp.concatenate([qg, flat(zin[h, mine, at, high])], axis=0)
            q, dout = qg[:, :dh], qg[:, dh:]
            yield
            raw = dot(keys, q, 1, 1)
            dprob = dot(values, dout, 1, 1)
            yield
            second = (i >= half).astype(jnp.int32) if both else 0
            src = c * chunk + ((i - second * half) >> 4)
            rank_q = ((own_at + second) * spots + src) * 2 + (i & 1)
            allowed = jnp.logical_and(cluster_k == cluster_q, rank_k <= rank_q)
            scores = jnp.where(allowed, raw * scale, NEGATIVE)
            w = jnp.exp(scores - jnp.max(scores, axis=0, keepdims=True))
            probs = w * (1.0 / jnp.sum(w, axis=0, keepdims=True))
            probs_half = probs.astype(BF16)
            delta = jnp.sum(probs * dprob, axis=0, keepdims=True)
            dscore = (probs * (dprob - delta)).astype(BF16)
            yield
            dq = (dot(dscore, keys, 0, 0) * scale).astype(BF16)
            attn = dot(probs_half, values, 0, 0).astype(BF16)
            more_k = dot(dscore, q, 1, 0)
            more_v = dot(probs_half, dout, 1, 0)
            dk = more_k if dk is None else dk + more_k
            dv = more_v if dv is None else dv + more_v
            yield
            for x, c0 in ((dq, two), (attn, two + dh)):
                send[h, mine, at, c0:c0 + dh] = x[:half].reshape(chunk, step, dh)
                if both:
                    zup[h, mine, at, c0:c0 + dh] = x[half:].reshape(chunk, step, dh)
        for x, c0 in (((dk * scale).astype(BF16), 0), (dv.astype(BF16), dh)):
            def cut(a):
                return x[a * quarter:(a + 1) * quarter].reshape(spots, step, dh)
            send[h, :, at, c0:c0 + dh] = cut(own_at)
            if nk > 1:
                zdown[h, :, at, c0:c0 + dh] = cut(0)
            if both:
                zdown[h, :, at, two + c0:two + c0 + dh] = cut(1)
                zup[h, :, at, c0:c0 + dh] = cut(3)

    together = 2 if tiles % 2 == 0 else 1

    def attend_all(h, nk, both):
        def some(g, carry):
            work = [attend(h, g * together + t, nk, both) for t in range(together)]
            while work:
                work = [w for w in work if next(w, True) is None]
            return carry
        lax.fori_loop(0, tiles // together, some, 0)

    def return_rows(h):
        for k in range(1, spots):
            back_copy(h, k).start()
        back[h, r] = send[h, r]

    def push(h):
        for k in range(1, spots):
            in_copy(h, k).wait_recv()

        @pl.when(z == 0)
        def _():
            kv_first(h).start()

        @pl.when(z == 1)
        def _():
            kv_own(h).start()

        @pl.when(z == 3)
        def _():
            top_down(h).start()

    def forward(h):
        @pl.when(z == 1)
        def _():
            kv_forward(h).wait_recv()
            kv_forward(h).start()

    def compute(h):
        for k in range(1, spots):
            out_copy(h, k).wait_send()

        @pl.when(z == 0)
        def _():
            attend_all(h, 1, False)

        @pl.when(z == 1)
        def _():
            attend_all(h, 2, False)

        @pl.when(z == 2)
        def _():
            kv_forward(h).wait_recv()
            kv_own(h).wait_recv()
            top_down(h).wait_recv()
            attend_all(h, 4, True)
            sums_down(h).start()
            top_back(h).start()
            return_rows(h)

    def give_back(h):
        @pl.when(z == 0)
        def _():
            last_down(h).wait_recv()
            send[h, :, :, low] = (send[h, :, :, low].astype(F32) + zin[h, :, :, low].astype(F32)).astype(BF16)

        @pl.when(z == 1)
        def _():
            sums_down(h).wait_recv()
            zdown[h, :, :, low] = (zdown[h, :, :, low].astype(F32) + zin[h, :, :, low].astype(F32)).astype(BF16)
            last_down(h).start()
            send[h, :, :, low] = (send[h, :, :, low].astype(F32) + zin[h, :, :, high].astype(F32)).astype(BF16)

        @pl.when(z == 3)
        def _():
            top_back(h).wait_recv()
            send[h] = zin[h]

        @pl.when(z != 2)
        def _():
            return_rows(h)

    def finish(h):
        cols = columns(h)
        for part in range(split):
            for k in range(1, spots):
                back_in(h * split + part, k).wait_recv()
        table = jnp.stack([back[h * split + part] for part in range(split)], axis=1).reshape(slots, four)
        rows_back = dot(onehot[h], table, 0, 0).astype(BF16)
        key_grad[:, cols] = rows_back[:, :dh]
        value_grad[:, cols] = rows_back[:, dh:two]
        query_grad[:, cols] = rows_back[:, two:two + dh]
        attn_all[:, cols] = rows_back[:, two + dh:]

        @pl.when(h % pair == pair - 1)
        def _():
            both = pl.ds(pl.multiple_of((h - (pair - 1)) * dh, pair * dh), pair * dh)
            total[...] += dot(attn_all[:, both], weight[both, :], 1, 0)

    pair = 2 if heads % 2 == 0 else 1

    def turn(t, carry):
        def stage(lag, run):
            @pl.when(jnp.logical_and(t >= lag, t < units + lag))
            def _():
                run(t - lag)

        @pl.when(jnp.logical_and(t < units, t % split == 0))
        def _():
            fill(t // split)

        stage(AHEAD, push)
        stage(AHEAD + 1, forward)
        stage(AHEAD + 2, compute)
        last = AHEAD + 2 + LAG + 1

        @pl.when(jnp.logical_and(t >= last, (t - last) % split == split - 1))
        def _():
            finish((t - last) // split)

        stage(AHEAD + 2 + LAG, give_back)
        return carry

    lax.fori_loop(0, units + AHEAD + LAG + 3, turn, 0)

    width = layer_out.shape[1]

    def share(k):
        return pltpu.make_async_remote_copy(
            src_ref=half_out.at[k - 1], dst_ref=half_in.at[k - 1],
            send_sem=hs.at[k - 1], recv_sem=hr.at[k - 1],
            device_id={"head": (hd + k) % nh}, device_id_type=MESH,
        )

    for k in range(1, nh):
        to = (hd + k) % nh
        half_out[k - 1] = total[:, pl.ds(pl.multiple_of(to * width, width), width)].astype(BF16)
        share(k).start()
    mine = total[:, pl.ds(pl.multiple_of(hd * width, width), width)]

    def settle(h, carry):
        for k in range(1, spots):
            back_copy(h, k).wait_send()

        @pl.when(z == 0)
        def _():
            kv_first(h).wait_send()

        @pl.when(z == 1)
        def _():
            kv_own(h).wait_send()
            kv_forward(h).wait_send()
            last_down(h).wait_send()

        @pl.when(z == 2)
        def _():
            sums_down(h).wait_send()
            top_back(h).wait_send()

        @pl.when(z == 3)
        def _():
            top_down(h).wait_send()

        return carry

    lax.fori_loop(0, units, settle, 0)
    for k in range(1, nh):
        share(k).wait()
        mine = mine + half_in[k - 1].astype(F32)
    layer_out[...] = mine.astype(BF16)


def hand_out(*refs):
    count = len(refs) // 2
    sems = refs[-1]
    parts = 4
    size = refs[0].shape[0] // parts
    copies = [
        pltpu.make_async_copy(
            refs[a].at[pl.ds(b * size, size)], refs[count + a].at[pl.ds(b * size, size)], sems.at[a, b]
        )
        for a in range(count)
        for b in range(parts)
    ]
    for copy in copies:
        copy.start()
    for copy in copies:
        copy.wait()


def body(nseq, nh, query_rows, key_rows, value_rows, out_grad, cluster_ids, out_weight):
    tokens, wide = query_rows.shape
    heads = cluster_ids.shape[0]
    dh = wide // heads
    spots = nseq // QUARTERS
    rows = CLUSTERS * MOST // spots
    split = 2 if rows % 32 == 0 else 1
    units = heads * split
    model = out_weight.shape[1]
    out = jax.ShapeDtypeStruct((tokens, wide), BF16)
    vm = pl.BlockSpec(memory_space=pltpu.VMEM)
    full = pltpu.VMEM((units, spots, rows // split, 4 * dh), BF16)
    dma = pltpu.SemaphoreType.DMA
    width = model // nh
    results = pl.pallas_call(
        functools.partial(kernel, spots, heads, split, dh, nh),
        out_shape=(jax.ShapeDtypeStruct((tokens, width), BF16), out, out, out),
        in_specs=[vm] * 6,
        out_specs=(vm,) * 4,
        scratch_shapes=[
            pltpu.VMEM((heads, CLUSTERS * MOST, tokens), BF16),
            pltpu.VMEM((tokens, tokens), BF16),
            pltpu.VMEM((tokens, wide), BF16),
            full, full, full, full, full, full, full,
            pltpu.VMEM((tokens, model), F32),
            pltpu.VMEM((nh - 1, tokens, width), BF16),
            pltpu.VMEM((nh - 1, tokens, width), BF16),
            dma((units, spots)), dma((units, spots)),
            dma((units, 2)), dma((units, 2)),
            dma((units, 2)), dma((units,)),
            dma((units, spots)), dma((units, spots)),
            dma((nh - 1,)), dma((nh - 1,)),
        ],
        compiler_params=pltpu.CompilerParams(
            collective_id=0, has_side_effects=True, vmem_limit_bytes=60 * 2**20
        ),
        cost_estimate=pl.CostEstimate(flops=10**10, bytes_accessed=2**24, transcendentals=2**21),
    )(
        query_rows, key_rows, value_rows, out_grad,
        cluster_ids.reshape(heads, 1, tokens), out_weight,
    )
    anywhere = pl.BlockSpec(memory_space=pl.ANY)
    return pl.pallas_call(
        hand_out,
        out_shape=tuple(jax.ShapeDtypeStruct(x.shape, x.dtype) for x in results),
        in_specs=[anywhere] * 4,
        out_specs=(anywhere,) * 4,
        scratch_shapes=[dma((4, 4))],
    )(*results)


def solution(mesh):
    in_specs = (
        P("seq", "head"),
        P("seq", "head"),
        P("seq", "head"),
        P("seq", None),
        P("head", "seq", None),
        P("head", None),
    )
    out_specs = (P("seq", "head"), P("seq", "head"), P("seq", "head"), P("seq", "head"))
    run = functools.partial(body, mesh.shape["seq"], mesh.shape["head"])
    return jax.shard_map(run, mesh=mesh, in_specs=in_specs, out_specs=out_specs, check_vma=False)
```

```python
import functools

import jax
import jax.numpy as jnp
from jax import lax
from jax.experimental import pallas as pl
from jax.experimental.pallas import tpu as pltpu
from jax.sharding import PartitionSpec as P

CLUSTERS = 256
MOST = 2
QUARTERS = 4
LAG = 6
AHEAD = 3
NEGATIVE = -1e30
MESH = pl.DeviceIdType.MESH
F32 = jnp.float32
BF16 = jnp.bfloat16


def dot(a, b, da, db):
    return lax.dot_general(a, b, (((da,), (db,)), ((), ())), preferred_element_type=F32)


def kernel(
    spots, heads, split, dh, nh,
    query, key, value, grad, ids_row, weight,
    layer_out, query_grad, key_grad, value_grad,
    onehot, earlier, attn_all, allow, send, got, kv, zin, zup, zdown, back, total, half_out, half_in,
    as_, ar, kvs, kvr, zs, zr, bs, br, hs, hr,
):
    tokens = query.shape[0]
    slots = CLUSTERS * MOST
    rows = slots // spots // split
    units = heads * split
    step = 16
    tiles = rows // step
    quarter = spots * step
    two = 2 * dh
    four = 4 * dh
    scale = dh ** -0.5
    seq = lax.axis_index("seq")
    hd = lax.axis_index("head")
    z = seq // spots
    r = seq % spots

    def peer(k):
        return z * spots + (r + k) % spots

    barrier = pltpu.get_barrier_semaphore()
    for k in range(1, spots):
        pl.semaphore_signal(barrier, inc=1, device_id={"seq": peer(k)}, device_id_type=MESH)
    for k in range(1, nh):
        pl.semaphore_signal(barrier, inc=1, device_id={"head": (hd + k) % nh}, device_id_type=MESH)

    whole = QUARTERS * spots
    for to in ((seq + spots) % whole, (seq + whole - spots) % whole):
        pl.semaphore_signal(barrier, inc=1, device_id={"seq": to}, device_id_type=MESH)
    pl.semaphore_wait(barrier, spots - 1 + nh - 1 + 2)

    def remote(src, dst, ss, rs, to):
        return pltpu.make_async_remote_copy(
            src_ref=src, dst_ref=dst, send_sem=ss, recv_sem=rs,
            device_id={"seq": to}, device_id_type=MESH,
        )

    def out_copy(h, k):
        d = (r + k) % spots
        return remote(send.at[h, d], got.at[h, r], as_.at[h, k], ar.at[h, k], peer(k))

    def in_copy(h, k):
        s = (r + spots - k) % spots
        return remote(send.at[h, s], got.at[h, s], as_.at[h, k], ar.at[h, k], peer(k))

    def back_copy(h, k):
        d = (r + k) % spots
        return remote(send.at[h, d], back.at[h, r], bs.at[h, k], br.at[h, k], peer(k))

    def back_in(h, k):
        s = (r + spots - k) % spots
        return remote(send.at[h, s], back.at[h, s], bs.at[h, k], br.at[h, k], peer(k))

    low = pl.ds(0, two)
    high = pl.ds(two, two)
    above = jnp.minimum(seq + spots, QUARTERS * spots - 1)
    below = jnp.maximum(seq - spots, 0)

    def kv_first(h):
        return remote(got.at[h, :, :, low], kv.at[h, :, :, low], kvs.at[h, 1], kvr.at[h, 0], above)

    def kv_own(h):
        return remote(got.at[h, :, :, low], kv.at[h, :, :, high], kvs.at[h, 1], kvr.at[h, 1], above)

    def kv_forward(h):
        return remote(kv.at[h, :, :, low], kv.at[h, :, :, low], kvs.at[h, 0], kvr.at[h, 0], above)

    def top_down(h):
        return remote(got.at[h], zin.at[h], zs.at[h, 0], zr.at[h], below)

    def top_back(h):
        return remote(zup.at[h], zin.at[h], zs.at[h, 0], zr.at[h], above)

    def sums_down(h):
        return remote(zdown.at[h], zin.at[h], zs.at[h, 1], zr.at[h], below)

    def last_down(h):
        return remote(zdown.at[h, :, :, low], zin.at[h, :, :, low], zs.at[h, 1], zr.at[h], below)

    def columns(h):
        return pl.ds(pl.multiple_of(h * dh, dh), dh)

    at0 = lax.broadcasted_iota(jnp.int32, (tokens, tokens), 0)
    at1 = lax.broadcasted_iota(jnp.int32, (tokens, tokens), 1)
    earlier[...] = jnp.where(at0 < at1, 1.0, 0.0).astype(BF16)

    def fill(h):
        cols = columns(h)
        row = ids_row[h]
        named = lax.broadcasted_iota(jnp.int32, (CLUSTERS, tokens), 0) == row
        counts = dot(jnp.where(named, 1.0, 0.0).astype(BF16), earlier[...], 1, 0)
        before = jnp.sum(jnp.where(named, counts, 0.0), axis=0, keepdims=True).astype(jnp.int32)
        slot = row * MOST + before
        place = lax.broadcasted_iota(jnp.int32, (slots, tokens), 0)
        picked = jnp.where(place == slot, 1.0, 0.0).astype(BF16)
        onehot[h] = picked
        attn_grad = dot(grad[...], weight[cols, :], 1, 1).astype(BF16)
        wide = jnp.concatenate([key[:, cols], value[:, cols], query[:, cols], attn_grad], axis=1)
        table = dot(picked, wide, 1, 0).astype(BF16).reshape(spots, split, rows, four)
        for part in range(split):
            u = h * split + part
            send[u] = table[:, part]
            for k in range(1, spots):
                out_copy(u, k).start()
            got[u, r] = send[u, r]

    total[...] = jnp.zeros_like(total)

    chunk = min(spots, 4)
    chunks = spots // chunk

    def flat(x):
        return x.reshape(x.shape[0] * step, x.shape[2])

    def causal(nkeys, nq, own_at, c):
        half = chunk * step
        j = lax.broadcasted_iota(jnp.int32, (nkeys, nq), 0)
        i = lax.broadcasted_iota(jnp.int32, (nkeys, nq), 1)
        second = (i >= half).astype(jnp.int32)
        src = c * chunk + ((i - second * half) >> 4)
        rank_q = ((own_at + second) * spots + src) * 2 + (i & 1)
        rank_k = (j >> 4) * 2 + (j & 1)
        same = ((j & 15) >> 1) == ((i & 15) >> 1)
        return jnp.where(jnp.logical_and(same, rank_k <= rank_q), 1.0, 0.0)

    if chunks == 1:
        allow[:, :2 * chunk * step] = causal(4 * quarter, 2 * chunk * step, 2, 0)

    def attend(h, g, nk, both):
        at = pl.ds(pl.multiple_of(g * step, step), step)
        own = flat(got[h, :, at, low])
        if both:
            parts = [flat(kv[h, :, at, low]), flat(kv[h, :, at, high]), own, flat(zin[h, :, at, low])]
        elif nk == 2:
            parts = [flat(kv[h, :, at, low]), own]
        else:
            parts = [own]
        kvs_all = jnp.concatenate(parts, axis=0) if nk > 1 else own
        keys, values = kvs_all[:, :dh], kvs_all[:, dh:]
        nkeys = nk * quarter
        half = chunk * step
        nq = half * (2 if both else 1)
        lit = jnp.where(keys != 0, 1, 0).astype(BF16)
        occupied = dot(lit, jnp.ones((dh, nq), BF16), 1, 0)
        own_at = nk - (2 if both else 1)
        dk = dv = None
        for c in range(chunks):
            mine = pl.ds(c * chunk, chunk)
            qg = flat(got[h, mine, at, high])
            if both:
                qg = jnp.concatenate([qg, flat(zin[h, mine, at, high])], axis=0)
            q, dout = qg[:, :dh], qg[:, dh:]
            yield
            raw = dot(keys, q, 1, 1)
            dprob = dot(values, dout, 1, 1)
            yield
            if chunks == 1:
                top = 0 if both else 3 - nk
                seen = allow[top * quarter:(top + nk) * quarter, :nq]
            else:
                seen = causal(nkeys, nq, own_at, c)
            scores = jnp.where(occupied * seen > 0, raw * scale, NEGATIVE)
            w = jnp.exp(scores - jnp.max(scores, axis=0, keepdims=True))
            probs = w * (1.0 / jnp.sum(w, axis=0, keepdims=True))
            probs_half = probs.astype(BF16)
            delta = jnp.sum(probs * dprob, axis=0, keepdims=True)
            dscore = (probs * (dprob - delta)).astype(BF16)
            yield
            dq = (dot(dscore, keys, 0, 0) * scale).astype(BF16)
            attn = dot(probs_half, values, 0, 0).astype(BF16)
            more_k = dot(dscore, q, 1, 0)
            more_v = dot(probs_half, dout, 1, 0)
            dk = more_k if dk is None else dk + more_k
            dv = more_v if dv is None else dv + more_v
            yield
            for x, c0 in ((dq, two), (attn, two + dh)):
                send[h, mine, at, c0:c0 + dh] = x[:half].reshape(chunk, step, dh)
                if both:
                    zup[h, mine, at, c0:c0 + dh] = x[half:].reshape(chunk, step, dh)
        for x, c0 in (((dk * scale).astype(BF16), 0), (dv.astype(BF16), dh)):
            def cut(a):
                return x[a * quarter:(a + 1) * quarter].reshape(spots, step, dh)
            send[h, :, at, c0:c0 + dh] = cut(own_at)
            if nk > 1:
                zdown[h, :, at, c0:c0 + dh] = cut(0)
            if both:
                zdown[h, :, at, two + c0:two + c0 + dh] = cut(1)
                zup[h, :, at, c0:c0 + dh] = cut(3)

    together = 2 if tiles % 2 == 0 else 1

    def attend_all(h, nk, both):
        def some(g, carry):
            work = [attend(h, g * together + t, nk, both) for t in range(together)]
            while work:
                work = [w for w in work if next(w, True) is None]
            return carry
        lax.fori_loop(0, tiles // together, some, 0)

    def return_rows(h):
        for k in range(1, spots):
            back_copy(h, k).start()
        back[h, r] = send[h, r]

    def push(h):
        for k in range(1, spots):
            in_copy(h, k).wait_recv()

        @pl.when(z == 0)
        def _():
            kv_first(h).start()

        @pl.when(z == 1)
        def _():
            kv_own(h).start()

        @pl.when(z == 3)
        def _():
            top_down(h).start()

    def forward(h):
        @pl.when(z == 1)
        def _():
            kv_forward(h).wait_recv()
            kv_forward(h).start()

    def compute(h):
        for k in range(1, spots):
            out_copy(h, k).wait_send()

        @pl.when(z == 0)
        def _():
            attend_all(h, 1, False)

        @pl.when(z == 1)
        def _():
            attend_all(h, 2, False)

        @pl.when(z == 2)
        def _():
            kv_forward(h).wait_recv()
            kv_own(h).wait_recv()
            top_down(h).wait_recv()
            attend_all(h, 4, True)
            sums_down(h).start()
            top_back(h).start()
            return_rows(h)

    def give_back(h):
        @pl.when(z == 0)
        def _():
            last_down(h).wait_recv()
            send[h, :, :, low] = (send[h, :, :, low].astype(F32) + zin[h, :, :, low].astype(F32)).astype(BF16)

        @pl.when(z == 1)
        def _():
            sums_down(h).wait_recv()
            zdown[h, :, :, low] = (zdown[h, :, :, low].astype(F32) + zin[h, :, :, low].astype(F32)).astype(BF16)
            last_down(h).start()
            send[h, :, :, low] = (send[h, :, :, low].astype(F32) + zin[h, :, :, high].astype(F32)).astype(BF16)

        @pl.when(z == 3)
        def _():
            top_back(h).wait_recv()
            send[h] = zin[h]

        @pl.when(z != 2)
        def _():
            return_rows(h)

    def finish(h):
        cols = columns(h)
        for part in range(split):
            for k in range(1, spots):
                back_in(h * split + part, k).wait_recv()
        table = jnp.stack([back[h * split + part] for part in range(split)], axis=1).reshape(slots, four)
        rows_back = dot(onehot[h], table, 0, 0).astype(BF16)
        key_grad[:, cols] = rows_back[:, :dh]
        value_grad[:, cols] = rows_back[:, dh:two]
        query_grad[:, cols] = rows_back[:, two:two + dh]
        attn_all[:, cols] = rows_back[:, two + dh:]

        @pl.when(h % pair == pair - 1)
        def _():
            both = pl.ds(pl.multiple_of((h - (pair - 1)) * dh, pair * dh), pair * dh)
            total[...] += dot(attn_all[:, both], weight[both, :], 1, 0)

    pair = 2 if heads % 2 == 0 else 1

    def turn(t, carry):
        def stage(lag, run):
            @pl.when(jnp.logical_and(t >= lag, t < units + lag))
            def _():
                run(t - lag)

        @pl.when(jnp.logical_and(t < units, t % split == 0))
        def _():
            fill(t // split)

        stage(AHEAD, push)
        stage(AHEAD + 1, forward)
        stage(AHEAD + 2, compute)
        last = AHEAD + 2 + LAG + 1

        @pl.when(jnp.logical_and(t >= last, (t - last) % split == split - 1))
        def _():
            finish((t - last) // split)

        stage(AHEAD + 2 + LAG, give_back)
        return carry

    lax.fori_loop(0, units + AHEAD + LAG + 3, turn, 0)

    width = layer_out.shape[1]

    def share(k):
        return pltpu.make_async_remote_copy(
            src_ref=half_out.at[k - 1], dst_ref=half_in.at[k - 1],
            send_sem=hs.at[k - 1], recv_sem=hr.at[k - 1],
            device_id={"head": (hd + k) % nh}, device_id_type=MESH,
        )

    for k in range(1, nh):
        to = (hd + k) % nh
        half_out[k - 1] = total[:, pl.ds(pl.multiple_of(to * width, width), width)].astype(BF16)
        share(k).start()
    mine = total[:, pl.ds(pl.multiple_of(hd * width, width), width)]

    def settle(h, carry):
        for k in range(1, spots):
            back_copy(h, k).wait_send()

        @pl.when(z == 0)
        def _():
            kv_first(h).wait_send()

        @pl.when(z == 1)
        def _():
            kv_own(h).wait_send()
            kv_forward(h).wait_send()
            last_down(h).wait_send()

        @pl.when(z == 2)
        def _():
            sums_down(h).wait_send()
            top_back(h).wait_send()

        @pl.when(z == 3)
        def _():
            top_down(h).wait_send()

        return carry

    lax.fori_loop(0, units, settle, 0)
    for k in range(1, nh):
        share(k).wait()
        mine = mine + half_in[k - 1].astype(F32)
    layer_out[...] = mine.astype(BF16)


def hand_out(*refs):
    count = len(refs) // 2
    for a in range(count):
        refs[count + a][...] = refs[a][...]


def body(nseq, nh, query_rows, key_rows, value_rows, out_grad, cluster_ids, out_weight):
    tokens, wide = query_rows.shape
    heads = cluster_ids.shape[0]
    dh = wide // heads
    spots = nseq // QUARTERS
    rows = CLUSTERS * MOST // spots
    split = 2 if rows % 32 == 0 else 1
    units = heads * split
    model = out_weight.shape[1]
    out = jax.ShapeDtypeStruct((tokens, wide), BF16)
    vm = pl.BlockSpec(memory_space=pltpu.VMEM)
    full = pltpu.VMEM((units, spots, rows // split, 4 * dh), BF16)
    dma = pltpu.SemaphoreType.DMA
    width = model // nh
    results = pl.pallas_call(
        functools.partial(kernel, spots, heads, split, dh, nh),
        out_shape=(jax.ShapeDtypeStruct((tokens, width), BF16), out, out, out),
        in_specs=[vm] * 6,
        out_specs=(vm,) * 4,
        scratch_shapes=[
            pltpu.VMEM((heads, CLUSTERS * MOST, tokens), BF16),
            pltpu.VMEM((tokens, tokens), BF16),
            pltpu.VMEM((tokens, wide), BF16),
            pltpu.VMEM((4 * 16 * spots, 128), F32) if spots <= 4 else pltpu.VMEM((8, 128), F32),
            full, full, full, full, full, full, full,
            pltpu.VMEM((tokens, model), F32),
            pltpu.VMEM((nh - 1, tokens, width), BF16),
            pltpu.VMEM((nh - 1, tokens, width), BF16),
            dma((units, spots)), dma((units, spots)),
            dma((units, 2)), dma((units, 2)),
            dma((units, 2)), dma((units,)),
            dma((units, spots)), dma((units, spots)),
            dma((nh - 1,)), dma((nh - 1,)),
        ],
        compiler_params=pltpu.CompilerParams(
            collective_id=0, has_side_effects=True, vmem_limit_bytes=60 * 2**20
        ),
        cost_estimate=pl.CostEstimate(flops=10**10, bytes_accessed=2**24, transcendentals=2**21),
    )(
        query_rows, key_rows, value_rows, out_grad,
        cluster_ids.reshape(heads, 1, tokens), out_weight,
    )
    blocks = [pl.BlockSpec((tokens // 4, x.shape[1]), lambda i: (i, 0)) for x in results]
    return pl.pallas_call(
        hand_out,
        grid=(4,),
        out_shape=tuple(jax.ShapeDtypeStruct(x.shape, x.dtype) for x in results),
        in_specs=blocks,
        out_specs=tuple(blocks),
        compiler_params=pltpu.CompilerParams(vmem_limit_bytes=16 * 2**20),
    )(*results)


def solution(mesh):
    in_specs = (
        P("seq", "head"),
        P("seq", "head"),
        P("seq", "head"),
        P("seq", None),
        P("head", "seq", None),
        P("head", None),
    )
    out_specs = (P("seq", "head"), P("seq", "head"), P("seq", "head"), P("seq", "head"))
    run = functools.partial(body, mesh.shape["seq"], mesh.shape["head"])
    return jax.shard_map(run, mesh=mesh, in_specs=in_specs, out_specs=out_specs, check_vma=False)
```

```python
import functools

import jax
import jax.numpy as jnp
from jax import lax
from jax.experimental import pallas as pl
from jax.experimental.pallas import tpu as pltpu
from jax.sharding import PartitionSpec as P

CLUSTERS = 256
MOST = 2
QUARTERS = 4
LAG = 6
LAG_LOWEST = 8
AHEAD = 3
NEGATIVE = -1e30
MESH = pl.DeviceIdType.MESH
F32 = jnp.float32
BF16 = jnp.bfloat16


def dot(a, b, da, db):
    return lax.dot_general(a, b, (((da,), (db,)), ((), ())), preferred_element_type=F32)


def kernel(
    spots, heads, split, dh, nh,
    query, key, value, grad, ids_row, weight,
    layer_out, query_grad, key_grad, value_grad,
    onehot, earlier, attn_all, allow, send, got, kv, zin, zup, zdown, back, total, half_out, half_in,
    as_, ar, kvs, kvr, zs, zr, bs, br, hs, hr,
):
    tokens = query.shape[0]
    slots = CLUSTERS * MOST
    rows = slots // spots // split
    units = heads * split
    step = 16
    tiles = rows // step
    quarter = spots * step
    two = 2 * dh
    four = 4 * dh
    scale = dh ** -0.5
    seq = lax.axis_index("seq")
    hd = lax.axis_index("head")
    z = seq // spots
    r = seq % spots

    def peer(k):
        return z * spots + (r + k) % spots

    barrier = pltpu.get_barrier_semaphore()
    for k in range(1, spots):
        pl.semaphore_signal(barrier, inc=1, device_id={"seq": peer(k)}, device_id_type=MESH)
    for k in range(1, nh):
        pl.semaphore_signal(barrier, inc=1, device_id={"head": (hd + k) % nh}, device_id_type=MESH)

    whole = QUARTERS * spots
    for to in ((seq + spots) % whole, (seq + whole - spots) % whole):
        pl.semaphore_signal(barrier, inc=1, device_id={"seq": to}, device_id_type=MESH)
    pl.semaphore_wait(barrier, spots - 1 + nh - 1 + 2)

    def remote(src, dst, ss, rs, to):
        return pltpu.make_async_remote_copy(
            src_ref=src, dst_ref=dst, send_sem=ss, recv_sem=rs,
            device_id={"seq": to}, device_id_type=MESH,
        )

    def out_copy(h, k):
        d = (r + k) % spots
        return remote(send.at[h, d], got.at[h, r], as_.at[h, k], ar.at[h, k], peer(k))

    def in_copy(h, k):
        s = (r + spots - k) % spots
        return remote(send.at[h, s], got.at[h, s], as_.at[h, k], ar.at[h, k], peer(k))

    def back_copy(h, k):
        d = (r + k) % spots
        return remote(send.at[h, d], back.at[h, r], bs.at[h, k], br.at[h, k], peer(k))

    def back_in(h, k):
        s = (r + spots - k) % spots
        return remote(send.at[h, s], back.at[h, s], bs.at[h, k], br.at[h, k], peer(k))

    low = pl.ds(0, two)
    high = pl.ds(two, two)
    above = jnp.minimum(seq + spots, QUARTERS * spots - 1)
    below = jnp.maximum(seq - spots, 0)

    def kv_first(h):
        return remote(got.at[h, :, :, low], kv.at[h, :, :, low], kvs.at[h, 1], kvr.at[h, 0], above)

    def kv_own(h):
        return remote(got.at[h, :, :, low], kv.at[h, :, :, high], kvs.at[h, 1], kvr.at[h, 1], above)

    def kv_forward(h):
        return remote(kv.at[h, :, :, low], kv.at[h, :, :, low], kvs.at[h, 0], kvr.at[h, 0], above)

    def top_down(h):
        return remote(got.at[h], zin.at[h], zs.at[h, 0], zr.at[h], below)

    def top_back(h):
        return remote(zup.at[h], zin.at[h], zs.at[h, 0], zr.at[h], above)

    def sums_down(h):
        return remote(zdown.at[h], zin.at[h], zs.at[h, 1], zr.at[h], below)

    def last_down(h):
        return remote(zdown.at[h, :, :, low], zin.at[h, :, :, low], zs.at[h, 1], zr.at[h], below)

    def columns(h):
        return pl.ds(pl.multiple_of(h * dh, dh), dh)

    at0 = lax.broadcasted_iota(jnp.int32, (tokens, tokens), 0)
    at1 = lax.broadcasted_iota(jnp.int32, (tokens, tokens), 1)
    earlier[...] = jnp.where(at0 < at1, 1.0, 0.0).astype(BF16)

    def fill(h):
        cols = columns(h)
        row = ids_row[h]
        named = lax.broadcasted_iota(jnp.int32, (CLUSTERS, tokens), 0) == row
        counts = dot(jnp.where(named, 1.0, 0.0).astype(BF16), earlier[...], 1, 0)
        before = jnp.sum(jnp.where(named, counts, 0.0), axis=0, keepdims=True).astype(jnp.int32)
        slot = row * MOST + before
        place = lax.broadcasted_iota(jnp.int32, (slots, tokens), 0)
        picked = jnp.where(place == slot, 1.0, 0.0).astype(BF16)
        onehot[h] = picked
        attn_grad = dot(grad[...], weight[cols, :], 1, 1).astype(BF16)
        wide = jnp.concatenate([key[:, cols], value[:, cols], query[:, cols], attn_grad], axis=1)
        table = dot(picked, wide, 1, 0).astype(BF16).reshape(spots, split, rows, four)
        for part in range(split):
            u = h * split + part
            send[u] = table[:, part]
            for k in range(1, spots):
                out_copy(u, k).start()
            got[u, r] = send[u, r]

    total[...] = jnp.zeros_like(total)

    chunk = min(spots, 4)
    chunks = spots // chunk

    def flat(x):
        return x.reshape(x.shape[0] * step, x.shape[2])

    def causal(nkeys, nq, own_at, c):
        half = chunk * step
        j = lax.broadcasted_iota(jnp.int32, (nkeys, nq), 0)
        i = lax.broadcasted_iota(jnp.int32, (nkeys, nq), 1)
        second = (i >= half).astype(jnp.int32)
        src = c * chunk + ((i - second * half) >> 4)
        rank_q = ((own_at + second) * spots + src) * 2 + (i & 1)
        rank_k = (j >> 4) * 2 + (j & 1)
        same = ((j & 15) >> 1) == ((i & 15) >> 1)
        return jnp.where(jnp.logical_and(same, rank_k <= rank_q), 1.0, 0.0)

    if chunks == 1:
        allow[:, :2 * chunk * step] = causal(4 * quarter, 2 * chunk * step, 2, 0)

    def attend(h, g, nk, both):
        at = pl.ds(pl.multiple_of(g * step, step), step)
        own = flat(got[h, :, at, low])
        if both:
            parts = [flat(kv[h, :, at, low]), flat(kv[h, :, at, high]), own, flat(zin[h, :, at, low])]
        elif nk == 2:
            parts = [flat(kv[h, :, at, low]), own]
        else:
            parts = [own]
        kvs_all = jnp.concatenate(parts, axis=0) if nk > 1 else own
        keys, values = kvs_all[:, :dh], kvs_all[:, dh:]
        nkeys = nk * quarter
        half = chunk * step
        nq = half * (2 if both else 1)
        lit = jnp.where(keys != 0, 1, 0).astype(BF16)
        occupied = dot(lit, jnp.ones((dh, nq), BF16), 1, 0)
        own_at = nk - (2 if both else 1)
        dk = dv = None
        for c in range(chunks):
            mine = pl.ds(c * chunk, chunk)
            qg = flat(got[h, mine, at, high])
            if both:
                qg = jnp.concatenate([qg, flat(zin[h, mine, at, high])], axis=0)
            q, dout = qg[:, :dh], qg[:, dh:]
            yield
            raw = dot(keys, q, 1, 1)
            dprob = dot(values, dout, 1, 1)
            yield
            if chunks == 1:
                top = 0 if both else 3 - nk
                seen = allow[top * quarter:(top + nk) * quarter, :nq]
            else:
                seen = causal(nkeys, nq, own_at, c)
            scores = jnp.where(occupied * seen > 0, raw * scale, NEGATIVE)
            w = jnp.exp(scores - jnp.max(scores, axis=0, keepdims=True))
            probs = w * (1.0 / jnp.sum(w, axis=0, keepdims=True))
            probs_half = probs.astype(BF16)
            delta = jnp.sum(probs * dprob, axis=0, keepdims=True)
            dscore = (probs * (dprob - delta)).astype(BF16)
            yield
            dq = (dot(dscore, keys, 0, 0) * scale).astype(BF16)
            attn = dot(probs_half, values, 0, 0).astype(BF16)
            more_k = dot(dscore, q, 1, 0)
            more_v = dot(probs_half, dout, 1, 0)
            dk = more_k if dk is None else dk + more_k
            dv = more_v if dv is None else dv + more_v
            yield
            for x, c0 in ((dq, two), (attn, two + dh)):
                send[h, mine, at, c0:c0 + dh] = x[:half].reshape(chunk, step, dh)
                if both:
                    zup[h, mine, at, c0:c0 + dh] = x[half:].reshape(chunk, step, dh)
        for x, c0 in (((dk * scale).astype(BF16), 0), (dv.astype(BF16), dh)):
            def cut(a):
                return x[a * quarter:(a + 1) * quarter].reshape(spots, step, dh)
            send[h, :, at, c0:c0 + dh] = cut(own_at)
            if nk > 1:
                zdown[h, :, at, c0:c0 + dh] = cut(0)
            if both:
                zdown[h, :, at, two + c0:two + c0 + dh] = cut(1)
                zup[h, :, at, c0:c0 + dh] = cut(3)

    together = 2 if tiles % 2 == 0 else 1

    def attend_all(h, nk, both):
        def some(g, carry):
            work = [attend(h, g * together + t, nk, both) for t in range(together)]
            while work:
                work = [w for w in work if next(w, True) is None]
            return carry
        lax.fori_loop(0, tiles // together, some, 0)

    def return_rows(h):
        for k in range(1, spots):
            back_copy(h, k).start()
        back[h, r] = send[h, r]

    def push(h):
        for k in range(1, spots):
            in_copy(h, k).wait_recv()

        @pl.when(z == 0)
        def _():
            kv_first(h).start()

        @pl.when(z == 1)
        def _():
            kv_own(h).start()

        @pl.when(z == 3)
        def _():
            top_down(h).start()

    def forward(h):
        @pl.when(z == 1)
        def _():
            kv_forward(h).wait_recv()
            kv_forward(h).start()

    def compute(h):
        for k in range(1, spots):
            out_copy(h, k).wait_send()

        @pl.when(z == 0)
        def _():
            attend_all(h, 1, False)

        @pl.when(z == 1)
        def _():
            attend_all(h, 2, False)

        @pl.when(z == 2)
        def _():
            kv_forward(h).wait_recv()
            kv_own(h).wait_recv()
            top_down(h).wait_recv()
            attend_all(h, 4, True)
            sums_down(h).start()
            top_back(h).start()
            return_rows(h)

    def give_back(h):
        @pl.when(z == 0)
        def _():
            last_down(h).wait_recv()
            send[h, :, :, low] = (send[h, :, :, low].astype(F32) + zin[h, :, :, low].astype(F32)).astype(BF16)

        @pl.when(z == 1)
        def _():
            sums_down(h).wait_recv()
            zdown[h, :, :, low] = (zdown[h, :, :, low].astype(F32) + zin[h, :, :, low].astype(F32)).astype(BF16)
            last_down(h).start()
            send[h, :, :, low] = (send[h, :, :, low].astype(F32) + zin[h, :, :, high].astype(F32)).astype(BF16)

        @pl.when(z == 3)
        def _():
            top_back(h).wait_recv()
            send[h] = zin[h]

        @pl.when(z != 2)
        def _():
            return_rows(h)

    def finish(h):
        cols = columns(h)
        for part in range(split):
            for k in range(1, spots):
                back_in(h * split + part, k).wait_recv()
        table = jnp.stack([back[h * split + part] for part in range(split)], axis=1).reshape(slots, four)
        rows_back = dot(onehot[h], table, 0, 0).astype(BF16)
        key_grad[:, cols] = rows_back[:, :dh]
        value_grad[:, cols] = rows_back[:, dh:two]
        query_grad[:, cols] = rows_back[:, two:two + dh]
        attn_all[:, cols] = rows_back[:, two + dh:]

        @pl.when(h % pair == pair - 1)
        def _():
            both = pl.ds(pl.multiple_of((h - (pair - 1)) * dh, pair * dh), pair * dh)
            total[...] += dot(attn_all[:, both], weight[both, :], 1, 0)

    pair = 2 if heads % 2 == 0 else 1

    def turn(t, carry):
        def stage(lag, run):
            @pl.when(jnp.logical_and(t >= lag, t < units + lag))
            def _():
                run(t - lag)

        @pl.when(jnp.logical_and(t < units, t % split == 0))
        def _():
            fill(t // split)

        stage(AHEAD, push)
        stage(AHEAD + 1, forward)
        stage(AHEAD + 2, compute)
        back_at = AHEAD + 2 + jnp.where(z == 0, LAG_LOWEST, LAG)
        done = t - back_at - 1

        @pl.when(jnp.logical_and(jnp.logical_and(done >= 0, done < units), done % split == split - 1))
        def _():
            finish(done // split)

        stage(back_at, give_back)
        return carry

    lax.fori_loop(0, units + AHEAD + LAG_LOWEST + 3, turn, 0)

    width = layer_out.shape[1]

    def share(k):
        return pltpu.make_async_remote_copy(
            src_ref=half_out.at[k - 1], dst_ref=half_in.at[k - 1],
            send_sem=hs.at[k - 1], recv_sem=hr.at[k - 1],
            device_id={"head": (hd + k) % nh}, device_id_type=MESH,
        )

    for k in range(1, nh):
        to = (hd + k) % nh
        half_out[k - 1] = total[:, pl.ds(pl.multiple_of(to * width, width), width)].astype(BF16)
        share(k).start()
    mine = total[:, pl.ds(pl.multiple_of(hd * width, width), width)]

    def settle(h, carry):
        for k in range(1, spots):
            back_copy(h, k).wait_send()

        @pl.when(z == 0)
        def _():
            kv_first(h).wait_send()

        @pl.when(z == 1)
        def _():
            kv_own(h).wait_send()
            kv_forward(h).wait_send()
            last_down(h).wait_send()

        @pl.when(z == 2)
        def _():
            sums_down(h).wait_send()
            top_back(h).wait_send()

        @pl.when(z == 3)
        def _():
            top_down(h).wait_send()

        return carry

    lax.fori_loop(0, units, settle, 0)
    for k in range(1, nh):
        share(k).wait()
        mine = mine + half_in[k - 1].astype(F32)
    layer_out[...] = mine.astype(BF16)


def hand_out(*refs):
    count = len(refs) // 2
    for a in range(count):
        refs[count + a][...] = refs[a][...]


def body(nseq, nh, query_rows, key_rows, value_rows, out_grad, cluster_ids, out_weight):
    tokens, wide = query_rows.shape
    heads = cluster_ids.shape[0]
    dh = wide // heads
    spots = nseq // QUARTERS
    rows = CLUSTERS * MOST // spots
    split = 2 if rows % 32 == 0 else 1
    units = heads * split
    model = out_weight.shape[1]
    out = jax.ShapeDtypeStruct((tokens, wide), BF16)
    vm = pl.BlockSpec(memory_space=pltpu.VMEM)
    full = pltpu.VMEM((units, spots, rows // split, 4 * dh), BF16)
    dma = pltpu.SemaphoreType.DMA
    width = model // nh
    results = pl.pallas_call(
        functools.partial(kernel, spots, heads, split, dh, nh),
        out_shape=(jax.ShapeDtypeStruct((tokens, width), BF16), out, out, out),
        in_specs=[vm] * 6,
        out_specs=(vm,) * 4,
        scratch_shapes=[
            pltpu.VMEM((heads, CLUSTERS * MOST, tokens), BF16),
            pltpu.VMEM((tokens, tokens), BF16),
            pltpu.VMEM((tokens, wide), BF16),
            pltpu.VMEM((4 * 16 * spots, 128), F32) if spots <= 4 else pltpu.VMEM((8, 128), F32),
            full, full, full, full, full, full, full,
            pltpu.VMEM((tokens, model), F32),
            pltpu.VMEM((nh - 1, tokens, width), BF16),
            pltpu.VMEM((nh - 1, tokens, width), BF16),
            dma((units, spots)), dma((units, spots)),
            dma((units, 2)), dma((units, 2)),
            dma((units, 2)), dma((units,)),
            dma((units, spots)), dma((units, spots)),
            dma((nh - 1,)), dma((nh - 1,)),
        ],
        compiler_params=pltpu.CompilerParams(
            collective_id=0, has_side_effects=True, vmem_limit_bytes=60 * 2**20
        ),
        cost_estimate=pl.CostEstimate(flops=10**10, bytes_accessed=2**24, transcendentals=2**21),
    )(
        query_rows, key_rows, value_rows, out_grad,
        cluster_ids.reshape(heads, 1, tokens), out_weight,
    )
    blocks = [pl.BlockSpec((tokens // 4, x.shape[1]), lambda i: (i, 0)) for x in results]
    return pl.pallas_call(
        hand_out,
        grid=(4,),
        out_shape=tuple(jax.ShapeDtypeStruct(x.shape, x.dtype) for x in results),
        in_specs=blocks,
        out_specs=tuple(blocks),
        compiler_params=pltpu.CompilerParams(vmem_limit_bytes=60 * 2**20),
    )(*results)


def solution(mesh):
    in_specs = (
        P("seq", "head"),
        P("seq", "head"),
        P("seq", "head"),
        P("seq", None),
        P("head", "seq", None),
        P("head", None),
    )
    out_specs = (P("seq", "head"), P("seq", "head"), P("seq", "head"), P("seq", "head"))
    run = functools.partial(body, mesh.shape["seq"], mesh.shape["head"])
    return jax.shard_map(run, mesh=mesh, in_specs=in_specs, out_specs=out_specs, check_vma=False)
```

```python
import functools

import jax
import jax.numpy as jnp
from jax import lax
from jax.experimental import pallas as pl
from jax.experimental.pallas import tpu as pltpu
from jax.sharding import PartitionSpec as P

CLUSTERS = 256
MOST = 2
QUARTERS = 4
LAG = 8
LAG_LOWEST = 11
AHEAD = 3
NEGATIVE = -1e30
MESH = pl.DeviceIdType.MESH
F32 = jnp.float32
BF16 = jnp.bfloat16


def dot(a, b, da, db):
    return lax.dot_general(a, b, (((da,), (db,)), ((), ())), preferred_element_type=F32)


def kernel(
    spots, heads, split, dh, nh,
    query, key, value, grad, ids_row, weight,
    layer_out, query_grad, key_grad, value_grad,
    onehot, earlier, attn_all, allow, send, got, kv, zin, zup, zdown, back, total, half_out, half_in,
    as_, ar, kvs, kvr, zs, zr, bs, br, hs, hr,
):
    tokens = query.shape[0]
    slots = CLUSTERS * MOST
    rows = slots // spots // split
    units = heads * split
    step = 16
    tiles = rows // step
    quarter = spots * step
    two = 2 * dh
    four = 4 * dh
    scale = dh ** -0.5
    seq = lax.axis_index("seq")
    hd = lax.axis_index("head")
    z = seq // spots
    r = seq % spots

    def peer(k):
        return z * spots + (r + k) % spots

    barrier = pltpu.get_barrier_semaphore()
    for k in range(1, spots):
        pl.semaphore_signal(barrier, inc=1, device_id={"seq": peer(k)}, device_id_type=MESH)
    for k in range(1, nh):
        pl.semaphore_signal(barrier, inc=1, device_id={"head": (hd + k) % nh}, device_id_type=MESH)

    whole = QUARTERS * spots
    for to in ((seq + spots) % whole, (seq + whole - spots) % whole):
        pl.semaphore_signal(barrier, inc=1, device_id={"seq": to}, device_id_type=MESH)
    pl.semaphore_wait(barrier, spots - 1 + nh - 1 + 2)

    def remote(src, dst, ss, rs, to):
        return pltpu.make_async_remote_copy(
            src_ref=src, dst_ref=dst, send_sem=ss, recv_sem=rs,
            device_id={"seq": to}, device_id_type=MESH,
        )

    def out_copy(h, k):
        d = (r + k) % spots
        return remote(send.at[h, d], got.at[h, r], as_.at[h, k], ar.at[h, k], peer(k))

    def in_copy(h, k):
        s = (r + spots - k) % spots
        return remote(send.at[h, s], got.at[h, s], as_.at[h, k], ar.at[h, k], peer(k))

    def back_copy(h, k):
        d = (r + k) % spots
        return remote(send.at[h, d], back.at[h, r], bs.at[h, k], br.at[h, k], peer(k))

    def back_in(h, k):
        s = (r + spots - k) % spots
        return remote(send.at[h, s], back.at[h, s], bs.at[h, k], br.at[h, k], peer(k))

    low = pl.ds(0, two)
    high = pl.ds(two, two)
    above = jnp.minimum(seq + spots, QUARTERS * spots - 1)
    below = jnp.maximum(seq - spots, 0)

    def kv_first(h):
        return remote(got.at[h, :, :, low], kv.at[h, :, :, low], kvs.at[h, 1], kvr.at[h, 0], above)

    def kv_own(h):
        return remote(got.at[h, :, :, low], kv.at[h, :, :, high], kvs.at[h, 1], kvr.at[h, 1], above)

    def kv_forward(h):
        return remote(kv.at[h, :, :, low], kv.at[h, :, :, low], kvs.at[h, 0], kvr.at[h, 0], above)

    def top_down(h):
        return remote(got.at[h], zin.at[h], zs.at[h, 0], zr.at[h], below)

    def top_back(h):
        return remote(zup.at[h], zin.at[h], zs.at[h, 0], zr.at[h], above)

    def sums_down(h):
        return remote(zdown.at[h], zin.at[h], zs.at[h, 1], zr.at[h], below)

    def last_down(h):
        return remote(zdown.at[h, :, :, low], zin.at[h, :, :, low], zs.at[h, 1], zr.at[h], below)

    def columns(h):
        return pl.ds(pl.multiple_of(h * dh, dh), dh)

    at0 = lax.broadcasted_iota(jnp.int32, (tokens, tokens), 0)
    at1 = lax.broadcasted_iota(jnp.int32, (tokens, tokens), 1)
    earlier[...] = jnp.where(at0 < at1, 1.0, 0.0).astype(BF16)

    def fill(h):
        cols = columns(h)
        row = ids_row[h]
        named = lax.broadcasted_iota(jnp.int32, (CLUSTERS, tokens), 0) == row
        counts = dot(jnp.where(named, 1.0, 0.0).astype(BF16), earlier[...], 1, 0)
        before = jnp.sum(jnp.where(named, counts, 0.0), axis=0, keepdims=True).astype(jnp.int32)
        slot = row * MOST + before
        place = lax.broadcasted_iota(jnp.int32, (slots, tokens), 0)
        picked = jnp.where(place == slot, 1.0, 0.0).astype(BF16)
        onehot[h] = picked
        attn_grad = dot(grad[...], weight[cols, :], 1, 1).astype(BF16)
        wide = jnp.concatenate([key[:, cols], value[:, cols], query[:, cols], attn_grad], axis=1)
        table = dot(picked, wide, 1, 0).astype(BF16).reshape(spots, split, rows, four)
        for part in range(split):
            u = h * split + part
            send[u] = table[:, part]
            for k in range(1, spots):
                out_copy(u, k).start()
            got[u, r] = send[u, r]

    total[...] = jnp.zeros_like(total)

    chunk = min(spots, 4)
    chunks = spots // chunk

    def flat(x):
        return x.reshape(x.shape[0] * step, x.shape[2])

    def causal(nkeys, nq, own_at, c):
        half = chunk * step
        j = lax.broadcasted_iota(jnp.int32, (nkeys, nq), 0)
        i = lax.broadcasted_iota(jnp.int32, (nkeys, nq), 1)
        second = (i >= half).astype(jnp.int32)
        src = c * chunk + ((i - second * half) >> 4)
        rank_q = ((own_at + second) * spots + src) * 2 + (i & 1)
        rank_k = (j >> 4) * 2 + (j & 1)
        same = ((j & 15) >> 1) == ((i & 15) >> 1)
        return jnp.where(jnp.logical_and(same, rank_k <= rank_q), 1.0, 0.0)

    if chunks == 1:
        allow[:, :2 * chunk * step] = causal(4 * quarter, 2 * chunk * step, 2, 0)

    def attend(h, g, nk, both):
        at = pl.ds(pl.multiple_of(g * step, step), step)
        own = flat(got[h, :, at, low])
        if both:
            parts = [flat(kv[h, :, at, low]), flat(kv[h, :, at, high]), own, flat(zin[h, :, at, low])]
        elif nk == 2:
            parts = [flat(kv[h, :, at, low]), own]
        else:
            parts = [own]
        kvs_all = jnp.concatenate(parts, axis=0) if nk > 1 else own
        keys, values = kvs_all[:, :dh], kvs_all[:, dh:]
        nkeys = nk * quarter
        half = chunk * step
        nq = half * (2 if both else 1)
        lit = jnp.where(keys != 0, 1, 0).astype(BF16)
        occupied = dot(lit, jnp.ones((dh, nq), BF16), 1, 0)
        own_at = nk - (2 if both else 1)
        dk = dv = None
        for c in range(chunks):
            mine = pl.ds(c * chunk, chunk)
            qg = flat(got[h, mine, at, high])
            if both:
                qg = jnp.concatenate([qg, flat(zin[h, mine, at, high])], axis=0)
            q, dout = qg[:, :dh], qg[:, dh:]
            yield
            raw = dot(keys, q, 1, 1)
            dprob = dot(values, dout, 1, 1)
            yield
            if chunks == 1:
                top = 0 if both else 3 - nk
                seen = allow[top * quarter:(top + nk) * quarter, :nq]
            else:
                seen = causal(nkeys, nq, own_at, c)
            scores = jnp.where(occupied * seen > 0, raw * scale, NEGATIVE)
            w = jnp.exp(scores - jnp.max(scores, axis=0, keepdims=True))
            probs = w * (1.0 / jnp.sum(w, axis=0, keepdims=True))
            probs_half = probs.astype(BF16)
            delta = jnp.sum(probs * dprob, axis=0, keepdims=True)
            dscore = (probs * (dprob - delta)).astype(BF16)
            yield
            dq = (dot(dscore, keys, 0, 0) * scale).astype(BF16)
            attn = dot(probs_half, values, 0, 0).astype(BF16)
            more_k = dot(dscore, q, 1, 0)
            more_v = dot(probs_half, dout, 1, 0)
            dk = more_k if dk is None else dk + more_k
            dv = more_v if dv is None else dv + more_v
            yield
            for x, c0 in ((dq, two), (attn, two + dh)):
                send[h, mine, at, c0:c0 + dh] = x[:half].reshape(chunk, step, dh)
                if both:
                    zup[h, mine, at, c0:c0 + dh] = x[half:].reshape(chunk, step, dh)
        for x, c0 in (((dk * scale).astype(BF16), 0), (dv.astype(BF16), dh)):
            def cut(a):
                return x[a * quarter:(a + 1) * quarter].reshape(spots, step, dh)
            send[h, :, at, c0:c0 + dh] = cut(own_at)
            if nk > 1:
                zdown[h, :, at, c0:c0 + dh] = cut(0)
            if both:
                zdown[h, :, at, two + c0:two + c0 + dh] = cut(1)
                zup[h, :, at, c0:c0 + dh] = cut(3)

    together = 2 if tiles % 2 == 0 else 1

    def attend_all(h, nk, both):
        def some(g, carry):
            work = [attend(h, g * together + t, nk, both) for t in range(together)]
            while work:
                work = [w for w in work if next(w, True) is None]
            return carry
        lax.fori_loop(0, tiles // together, some, 0)

    def return_rows(h):
        for k in range(1, spots):
            back_copy(h, k).start()
        back[h, r] = send[h, r]

    def push(h):
        for k in range(1, spots):
            in_copy(h, k).wait_recv()

        @pl.when(z == 0)
        def _():
            kv_first(h).start()

        @pl.when(z == 1)
        def _():
            kv_own(h).start()

        @pl.when(z == 3)
        def _():
            top_down(h).start()

    def forward(h):
        @pl.when(z == 1)
        def _():
            kv_forward(h).wait_recv()
            kv_forward(h).start()

    def compute(h):
        for k in range(1, spots):
            out_copy(h, k).wait_send()

        @pl.when(z == 0)
        def _():
            attend_all(h, 1, False)

        @pl.when(z == 1)
        def _():
            attend_all(h, 2, False)

        @pl.when(z == 2)
        def _():
            kv_forward(h).wait_recv()
            kv_own(h).wait_recv()
            top_down(h).wait_recv()
            attend_all(h, 4, True)
            sums_down(h).start()
            top_back(h).start()
            return_rows(h)

    def give_back(h):
        @pl.when(z == 0)
        def _():
            last_down(h).wait_recv()
            send[h, :, :, low] = (send[h, :, :, low].astype(F32) + zin[h, :, :, low].astype(F32)).astype(BF16)

        @pl.when(z == 1)
        def _():
            sums_down(h).wait_recv()
            zdown[h, :, :, low] = (zdown[h, :, :, low].astype(F32) + zin[h, :, :, low].astype(F32)).astype(BF16)
            last_down(h).start()
            send[h, :, :, low] = (send[h, :, :, low].astype(F32) + zin[h, :, :, high].astype(F32)).astype(BF16)

        @pl.when(z == 3)
        def _():
            top_back(h).wait_recv()
            send[h] = zin[h]

        @pl.when(z != 2)
        def _():
            return_rows(h)

    def finish(h):
        cols = columns(h)
        for part in range(split):
            for k in range(1, spots):
                back_in(h * split + part, k).wait_recv()
        table = jnp.stack([back[h * split + part] for part in range(split)], axis=1).reshape(slots, four)
        rows_back = dot(onehot[h], table, 0, 0).astype(BF16)
        key_grad[:, cols] = rows_back[:, :dh]
        value_grad[:, cols] = rows_back[:, dh:two]
        query_grad[:, cols] = rows_back[:, two:two + dh]
        attn_all[:, cols] = rows_back[:, two + dh:]

        @pl.when(h % pair == pair - 1)
        def _():
            both = pl.ds(pl.multiple_of((h - (pair - 1)) * dh, pair * dh), pair * dh)
            total[...] += dot(attn_all[:, both], weight[both, :], 1, 0)

    pair = 2 if heads % 2 == 0 else 1

    def turn(t, carry):
        def stage(lag, run):
            @pl.when(jnp.logical_and(t >= lag, t < units + lag))
            def _():
                run(t - lag)

        @pl.when(jnp.logical_and(t < units, t % split == 0))
        def _():
            fill(t // split)

        stage(AHEAD, push)
        stage(AHEAD + 1, forward)
        stage(AHEAD + 2, compute)
        back_at = AHEAD + 2 + jnp.where(z == 0, LAG_LOWEST, LAG)
        done = t - back_at - 1

        @pl.when(jnp.logical_and(jnp.logical_and(done >= 0, done < units), done % split == split - 1))
        def _():
            finish(done // split)

        stage(back_at, give_back)
        return carry

    lax.fori_loop(0, units + AHEAD + LAG_LOWEST + 3, turn, 0)

    width = layer_out.shape[1]

    def share(k):
        return pltpu.make_async_remote_copy(
            src_ref=half_out.at[k - 1], dst_ref=half_in.at[k - 1],
            send_sem=hs.at[k - 1], recv_sem=hr.at[k - 1],
            device_id={"head": (hd + k) % nh}, device_id_type=MESH,
        )

    for k in range(1, nh):
        to = (hd + k) % nh
        half_out[k - 1] = total[:, pl.ds(pl.multiple_of(to * width, width), width)].astype(BF16)
        share(k).start()
    mine = total[:, pl.ds(pl.multiple_of(hd * width, width), width)]

    def settle(h, carry):
        for k in range(1, spots):
            back_copy(h, k).wait_send()

        @pl.when(z == 0)
        def _():
            kv_first(h).wait_send()

        @pl.when(z == 1)
        def _():
            kv_own(h).wait_send()
            kv_forward(h).wait_send()
            last_down(h).wait_send()

        @pl.when(z == 2)
        def _():
            sums_down(h).wait_send()
            top_back(h).wait_send()

        @pl.when(z == 3)
        def _():
            top_down(h).wait_send()

        return carry

    lax.fori_loop(0, units, settle, 0)
    for k in range(1, nh):
        share(k).wait()
        mine = mine + half_in[k - 1].astype(F32)
    layer_out[...] = mine.astype(BF16)


def hand_out(*refs):
    count = len(refs) // 2
    for a in range(count):
        refs[count + a][...] = refs[a][...]


def body(nseq, nh, query_rows, key_rows, value_rows, out_grad, cluster_ids, out_weight):
    tokens, wide = query_rows.shape
    heads = cluster_ids.shape[0]
    dh = wide // heads
    spots = nseq // QUARTERS
    rows = CLUSTERS * MOST // spots
    split = max(s for s in (1, 2, 4) if rows % (16 * s) == 0)
    units = heads * split
    model = out_weight.shape[1]
    out = jax.ShapeDtypeStruct((tokens, wide), BF16)
    vm = pl.BlockSpec(memory_space=pltpu.VMEM)
    full = pltpu.VMEM((units, spots, rows // split, 4 * dh), BF16)
    dma = pltpu.SemaphoreType.DMA
    width = model // nh
    results = pl.pallas_call(
        functools.partial(kernel, spots, heads, split, dh, nh),
        out_shape=(jax.ShapeDtypeStruct((tokens, width), BF16), out, out, out),
        in_specs=[vm] * 6,
        out_specs=(vm,) * 4,
        scratch_shapes=[
            pltpu.VMEM((heads, CLUSTERS * MOST, tokens), BF16),
            pltpu.VMEM((tokens, tokens), BF16),
            pltpu.VMEM((tokens, wide), BF16),
            pltpu.VMEM((4 * 16 * spots, 128), F32) if spots <= 4 else pltpu.VMEM((8, 128), F32),
            full, full, full, full, full, full, full,
            pltpu.VMEM((tokens, model), F32),
            pltpu.VMEM((nh - 1, tokens, width), BF16),
            pltpu.VMEM((nh - 1, tokens, width), BF16),
            dma((units, spots)), dma((units, spots)),
            dma((units, 2)), dma((units, 2)),
            dma((units, 2)), dma((units,)),
            dma((units, spots)), dma((units, spots)),
            dma((nh - 1,)), dma((nh - 1,)),
        ],
        compiler_params=pltpu.CompilerParams(
            collective_id=0, has_side_effects=True, vmem_limit_bytes=60 * 2**20
        ),
        cost_estimate=pl.CostEstimate(flops=10**10, bytes_accessed=2**24, transcendentals=2**21),
    )(
        query_rows, key_rows, value_rows, out_grad,
        cluster_ids.reshape(heads, 1, tokens), out_weight,
    )
    blocks = [pl.BlockSpec((tokens // 4, x.shape[1]), lambda i: (i, 0)) for x in results]
    return pl.pallas_call(
        hand_out,
        grid=(4,),
        out_shape=tuple(jax.ShapeDtypeStruct(x.shape, x.dtype) for x in results),
        in_specs=blocks,
        out_specs=tuple(blocks),
        compiler_params=pltpu.CompilerParams(vmem_limit_bytes=60 * 2**20),
    )(*results)


def solution(mesh):
    in_specs = (
        P("seq", "head"),
        P("seq", "head"),
        P("seq", "head"),
        P("seq", None),
        P("head", "seq", None),
        P("head", None),
    )
    out_specs = (P("seq", "head"), P("seq", "head"), P("seq", "head"), P("seq", "head"))
    run = functools.partial(body, mesh.shape["seq"], mesh.shape["head"])
    return jax.shard_map(run, mesh=mesh, in_specs=in_specs, out_specs=out_specs, check_vma=False)
```

```python
import functools

import jax
import jax.numpy as jnp
from jax import lax
from jax.experimental import pallas as pl
from jax.experimental.pallas import tpu as pltpu
from jax.sharding import PartitionSpec as P

CLUSTERS = 256
MOST = 2
QUARTERS = 4
LAG = 8
LAG_LOWEST = 11
AHEAD = 3
NEGATIVE = -1e30
MESH = pl.DeviceIdType.MESH
F32 = jnp.float32
BF16 = jnp.bfloat16


def dot(a, b, da, db):
    return lax.dot_general(a, b, (((da,), (db,)), ((), ())), preferred_element_type=F32)


def kernel(
    spots, heads, split, dh, nh,
    query, key, value, grad, ids_row, weight,
    layer_out, query_grad, key_grad, value_grad,
    onehot, earlier, attn_all, allow, send, got, kv, zin, zup, zdown, back, total, half_out, half_in,
    as_, ar, kvs, kvr, zs, zr, bs, br, hs, hr,
):
    tokens = query.shape[0]
    slots = CLUSTERS * MOST
    rows = slots // spots // split
    units = heads * split
    step = 16
    tiles = rows // step
    quarter = spots * step
    two = 2 * dh
    four = 4 * dh
    scale = dh ** -0.5
    seq = lax.axis_index("seq")
    hd = lax.axis_index("head")
    z = seq // spots
    r = seq % spots

    def peer(k):
        return z * spots + (r + k) % spots

    barrier = pltpu.get_barrier_semaphore()
    for k in range(1, spots):
        pl.semaphore_signal(barrier, inc=1, device_id={"seq": peer(k)}, device_id_type=MESH)
    for k in range(1, nh):
        pl.semaphore_signal(barrier, inc=1, device_id={"head": (hd + k) % nh}, device_id_type=MESH)

    whole = QUARTERS * spots
    for to in ((seq + spots) % whole, (seq + whole - spots) % whole):
        pl.semaphore_signal(barrier, inc=1, device_id={"seq": to}, device_id_type=MESH)
    pl.semaphore_wait(barrier, spots - 1 + nh - 1 + 2)

    def remote(src, dst, ss, rs, to):
        return pltpu.make_async_remote_copy(
            src_ref=src, dst_ref=dst, send_sem=ss, recv_sem=rs,
            device_id={"seq": to}, device_id_type=MESH,
        )

    def out_copy(h, k):
        d = (r + k) % spots
        return remote(send.at[h, d], got.at[h, r], as_.at[h, k], ar.at[h, k], peer(k))

    def in_copy(h, k):
        s = (r + spots - k) % spots
        return remote(send.at[h, s], got.at[h, s], as_.at[h, k], ar.at[h, k], peer(k))

    def back_copy(h, k):
        d = (r + k) % spots
        return remote(send.at[h, d], back.at[h, r], bs.at[h, k], br.at[h, k], peer(k))

    def back_in(h, k):
        s = (r + spots - k) % spots
        return remote(send.at[h, s], back.at[h, s], bs.at[h, k], br.at[h, k], peer(k))

    low = pl.ds(0, two)
    high = pl.ds(two, two)
    above = jnp.minimum(seq + spots, QUARTERS * spots - 1)
    below = jnp.maximum(seq - spots, 0)

    def kv_first(h):
        return remote(got.at[h, :, :, low], kv.at[h, :, :, low], kvs.at[h, 1], kvr.at[h, 0], above)

    def kv_own(h):
        return remote(got.at[h, :, :, low], kv.at[h, :, :, high], kvs.at[h, 1], kvr.at[h, 1], above)

    def kv_forward(h):
        return remote(kv.at[h, :, :, low], kv.at[h, :, :, low], kvs.at[h, 0], kvr.at[h, 0], above)

    def top_down(h):
        return remote(got.at[h], zin.at[h], zs.at[h, 0], zr.at[h], below)

    def top_back(h):
        return remote(zup.at[h], zin.at[h], zs.at[h, 0], zr.at[h], above)

    def sums_down(h):
        return remote(zdown.at[h], zin.at[h], zs.at[h, 1], zr.at[h], below)

    def last_down(h):
        return remote(zdown.at[h, :, :, low], zin.at[h, :, :, low], zs.at[h, 1], zr.at[h], below)

    def columns(h):
        return pl.ds(pl.multiple_of(h * dh, dh), dh)

    at0 = lax.broadcasted_iota(jnp.int32, (tokens, tokens), 0)
    at1 = lax.broadcasted_iota(jnp.int32, (tokens, tokens), 1)
    earlier[...] = jnp.where(at0 < at1, 1.0, 0.0).astype(BF16)

    def fill(h):
        cols = columns(h)
        row = ids_row[h]
        named = lax.broadcasted_iota(jnp.int32, (CLUSTERS, tokens), 0) == row
        counts = dot(jnp.where(named, 1.0, 0.0).astype(BF16), earlier[...], 1, 0)
        before = jnp.sum(jnp.where(named, counts, 0.0), axis=0, keepdims=True).astype(jnp.int32)
        slot = row * MOST + before
        place = lax.broadcasted_iota(jnp.int32, (slots, tokens), 0)
        picked = jnp.where(place == slot, 1.0, 0.0).astype(BF16)
        onehot[h] = picked
        attn_grad = dot(grad[...], weight[cols, :], 1, 1).astype(BF16)
        wide = jnp.concatenate([key[:, cols], value[:, cols], query[:, cols], attn_grad], axis=1)
        table = dot(picked, wide, 1, 0).astype(BF16).reshape(spots, split, rows, four)
        for part in range(split):
            u = h * split + part
            send[u] = table[:, part]
            for k in range(1, spots):
                out_copy(u, k).start()
            got[u, r] = send[u, r]

    total[...] = jnp.zeros_like(total)

    chunk = min(spots, 4)
    chunks = spots // chunk

    def flat(x):
        return x.reshape(x.shape[0] * step, x.shape[2])

    def causal(nkeys, nq, own_at, c):
        half = chunk * step
        j = lax.broadcasted_iota(jnp.int32, (nkeys, nq), 0)
        i = lax.broadcasted_iota(jnp.int32, (nkeys, nq), 1)
        second = (i >= half).astype(jnp.int32)
        src = c * chunk + ((i - second * half) >> 4)
        rank_q = ((own_at + second) * spots + src) * 2 + (i & 1)
        rank_k = (j >> 4) * 2 + (j & 1)
        same = ((j & 15) >> 1) == ((i & 15) >> 1)
        return jnp.where(jnp.logical_and(same, rank_k <= rank_q), 1.0, 0.0)

    if chunks == 1:
        allow[:, :2 * chunk * step] = causal(4 * quarter, 2 * chunk * step, 2, 0)

    def attend(h, g, nk, both):
        at = pl.ds(pl.multiple_of(g * step, step), step)
        own = flat(got[h, :, at, low])
        if both:
            parts = [flat(kv[h, :, at, low]), flat(kv[h, :, at, high]), own, flat(zin[h, :, at, low])]
        elif nk == 2:
            parts = [flat(kv[h, :, at, low]), own]
        else:
            parts = [own]
        kvs_all = jnp.concatenate(parts, axis=0) if nk > 1 else own
        keys, values = kvs_all[:, :dh], kvs_all[:, dh:]
        nkeys = nk * quarter
        half = chunk * step
        nq = half * (2 if both else 1)
        lit = jnp.where(keys != 0, 1, 0).astype(BF16)
        occupied = dot(lit, jnp.ones((dh, nq), BF16), 1, 0)
        own_at = nk - (2 if both else 1)
        dk = dv = None
        for c in range(chunks):
            mine = pl.ds(c * chunk, chunk)
            qg = flat(got[h, mine, at, high])
            if both:
                qg = jnp.concatenate([qg, flat(zin[h, mine, at, high])], axis=0)
            q, dout = qg[:, :dh], qg[:, dh:]
            yield
            raw = dot(keys, q, 1, 1)
            dprob = dot(values, dout, 1, 1)
            yield
            if chunks == 1:
                top = 0 if both else 3 - nk
                seen = allow[top * quarter:(top + nk) * quarter, :nq]
            else:
                seen = causal(nkeys, nq, own_at, c)
            scores = jnp.where(occupied * seen > 0, raw * scale, NEGATIVE)
            w = jnp.exp(scores - jnp.max(scores, axis=0, keepdims=True))
            probs = w * (1.0 / jnp.sum(w, axis=0, keepdims=True))
            probs_half = probs.astype(BF16)
            delta = jnp.sum(probs * dprob, axis=0, keepdims=True)
            dscore = (probs * (dprob - delta)).astype(BF16)
            yield
            dq = (dot(dscore, keys, 0, 0) * scale).astype(BF16)
            attn = dot(probs_half, values, 0, 0).astype(BF16)
            more_k = dot(dscore, q, 1, 0)
            more_v = dot(probs_half, dout, 1, 0)
            dk = more_k if dk is None else dk + more_k
            dv = more_v if dv is None else dv + more_v
            yield
            for x, c0 in ((dq, two), (attn, two + dh)):
                send[h, mine, at, c0:c0 + dh] = x[:half].reshape(chunk, step, dh)
                if both:
                    zup[h, mine, at, c0:c0 + dh] = x[half:].reshape(chunk, step, dh)
        for x, c0 in (((dk * scale).astype(BF16), 0), (dv.astype(BF16), dh)):
            def cut(a):
                return x[a * quarter:(a + 1) * quarter].reshape(spots, step, dh)
            send[h, :, at, c0:c0 + dh] = cut(own_at)
            if nk > 1:
                zdown[h, :, at, c0:c0 + dh] = cut(0)
            if both:
                zdown[h, :, at, two + c0:two + c0 + dh] = cut(1)
                zup[h, :, at, c0:c0 + dh] = cut(3)

    together = 2 if tiles % 2 == 0 else 1

    def attend_all(h, nk, both):
        def some(g, carry):
            work = [attend(h, g * together + t, nk, both) for t in range(together)]
            while work:
                work = [w for w in work if next(w, True) is None]
            return carry
        lax.fori_loop(0, tiles // together, some, 0)

    def return_rows(h):
        for k in range(1, spots):
            back_copy(h, k).start()
        back[h, r] = send[h, r]

    def push(h):
        for k in range(1, spots):
            in_copy(h, k).wait_recv()

        @pl.when(z == 0)
        def _():
            kv_first(h).start()

        @pl.when(z == 1)
        def _():
            kv_own(h).start()

        @pl.when(z == 3)
        def _():
            top_down(h).start()

    def forward(h):
        @pl.when(z == 1)
        def _():
            kv_forward(h).wait_recv()
            kv_forward(h).start()

    def compute(h):
        for k in range(1, spots):
            out_copy(h, k).wait_send()

        @pl.when(z == 0)
        def _():
            attend_all(h, 1, False)

        @pl.when(z == 1)
        def _():
            attend_all(h, 2, False)

        @pl.when(z == 2)
        def _():
            kv_forward(h).wait_recv()
            kv_own(h).wait_recv()
            top_down(h).wait_recv()
            attend_all(h, 4, True)
            sums_down(h).start()
            top_back(h).start()
            return_rows(h)

    def give_back(h):
        @pl.when(z == 0)
        def _():
            last_down(h).wait_recv()
            send[h, :, :, low] = (send[h, :, :, low].astype(F32) + zin[h, :, :, low].astype(F32)).astype(BF16)

        @pl.when(z == 1)
        def _():
            sums_down(h).wait_recv()
            zdown[h, :, :, low] = (zdown[h, :, :, low].astype(F32) + zin[h, :, :, low].astype(F32)).astype(BF16)
            last_down(h).start()
            send[h, :, :, low] = (send[h, :, :, low].astype(F32) + zin[h, :, :, high].astype(F32)).astype(BF16)

        @pl.when(z == 3)
        def _():
            top_back(h).wait_recv()
            send[h] = zin[h]

        @pl.when(z != 2)
        def _():
            return_rows(h)

    def finish(h):
        cols = columns(h)
        for part in range(split):
            for k in range(1, spots):
                back_in(h * split + part, k).wait_recv()
        table = jnp.stack([back[h * split + part] for part in range(split)], axis=1).reshape(slots, four)
        rows_back = dot(onehot[h], table, 0, 0).astype(BF16)
        key_grad[:, cols] = rows_back[:, :dh]
        value_grad[:, cols] = rows_back[:, dh:two]
        query_grad[:, cols] = rows_back[:, two:two + dh]
        attn_all[:, cols] = rows_back[:, two + dh:]

        @pl.when(h % pair == pair - 1)
        def _():
            both = pl.ds(pl.multiple_of((h - (pair - 1)) * dh, pair * dh), pair * dh)
            total[...] += dot(attn_all[:, both], weight[both, :], 1, 0)

    pair = 2 if heads % 2 == 0 else 1

    def turn(t, carry):
        def stage(lag, run):
            @pl.when(jnp.logical_and(t >= lag, t < units + lag))
            def _():
                run(t - lag)

        @pl.when(jnp.logical_and(t < units, t % split == 0))
        def _():
            fill(t // split)

        stage(AHEAD + 1, forward)
        stage(AHEAD, push)
        stage(AHEAD + 2, compute)
        back_at = AHEAD + 2 + jnp.where(z == 0, LAG_LOWEST, LAG)
        done = t - back_at - 1

        @pl.when(jnp.logical_and(jnp.logical_and(done >= 0, done < units), done % split == split - 1))
        def _():
            finish(done // split)

        stage(back_at, give_back)
        return carry

    lax.fori_loop(0, units + AHEAD + LAG_LOWEST + 3, turn, 0)

    width = layer_out.shape[1]

    def share(k):
        return pltpu.make_async_remote_copy(
            src_ref=half_out.at[k - 1], dst_ref=half_in.at[k - 1],
            send_sem=hs.at[k - 1], recv_sem=hr.at[k - 1],
            device_id={"head": (hd + k) % nh}, device_id_type=MESH,
        )

    for k in range(1, nh):
        to = (hd + k) % nh
        half_out[k - 1] = total[:, pl.ds(pl.multiple_of(to * width, width), width)].astype(BF16)
        share(k).start()
    mine = total[:, pl.ds(pl.multiple_of(hd * width, width), width)]

    def settle(h, carry):
        for k in range(1, spots):
            back_copy(h, k).wait_send()

        @pl.when(z == 0)
        def _():
            kv_first(h).wait_send()

        @pl.when(z == 1)
        def _():
            kv_own(h).wait_send()
            kv_forward(h).wait_send()
            last_down(h).wait_send()

        @pl.when(z == 2)
        def _():
            sums_down(h).wait_send()
            top_back(h).wait_send()

        @pl.when(z == 3)
        def _():
            top_down(h).wait_send()

        return carry

    lax.fori_loop(0, units, settle, 0)
    for k in range(1, nh):
        share(k).wait()
        mine = mine + half_in[k - 1].astype(F32)
    layer_out[...] = mine.astype(BF16)


def hand_out(*refs):
    count = len(refs) // 2
    for a in range(count):
        refs[count + a][...] = refs[a][...]


def body(nseq, nh, query_rows, key_rows, value_rows, out_grad, cluster_ids, out_weight):
    tokens, wide = query_rows.shape
    heads = cluster_ids.shape[0]
    dh = wide // heads
    spots = nseq // QUARTERS
    rows = CLUSTERS * MOST // spots
    split = max(s for s in (1, 2, 4) if rows % (16 * s) == 0)
    units = heads * split
    model = out_weight.shape[1]
    out = jax.ShapeDtypeStruct((tokens, wide), BF16)
    vm = pl.BlockSpec(memory_space=pltpu.VMEM)
    full = pltpu.VMEM((units, spots, rows // split, 4 * dh), BF16)
    dma = pltpu.SemaphoreType.DMA
    width = model // nh
    results = pl.pallas_call(
        functools.partial(kernel, spots, heads, split, dh, nh),
        out_shape=(jax.ShapeDtypeStruct((tokens, width), BF16), out, out, out),
        in_specs=[vm] * 6,
        out_specs=(vm,) * 4,
        scratch_shapes=[
            pltpu.VMEM((heads, CLUSTERS * MOST, tokens), BF16),
            pltpu.VMEM((tokens, tokens), BF16),
            pltpu.VMEM((tokens, wide), BF16),
            pltpu.VMEM((4 * 16 * spots, 128), F32) if spots <= 4 else pltpu.VMEM((8, 128), F32),
            full, full, full, full, full, full, full,
            pltpu.VMEM((tokens, model), F32),
            pltpu.VMEM((nh - 1, tokens, width), BF16),
            pltpu.VMEM((nh - 1, tokens, width), BF16),
            dma((units, spots)), dma((units, spots)),
            dma((units, 2)), dma((units, 2)),
            dma((units, 2)), dma((units,)),
            dma((units, spots)), dma((units, spots)),
            dma((nh - 1,)), dma((nh - 1,)),
        ],
        compiler_params=pltpu.CompilerParams(
            collective_id=0, has_side_effects=True, vmem_limit_bytes=60 * 2**20
        ),
        cost_estimate=pl.CostEstimate(flops=10**10, bytes_accessed=2**24, transcendentals=2**21),
    )(
        query_rows, key_rows, value_rows, out_grad,
        cluster_ids.reshape(heads, 1, tokens), out_weight,
    )
    blocks = [pl.BlockSpec((tokens // 8, x.shape[1]), lambda i: (i, 0)) for x in results]
    return pl.pallas_call(
        hand_out,
        grid=(8,),
        out_shape=tuple(jax.ShapeDtypeStruct(x.shape, x.dtype) for x in results),
        in_specs=blocks,
        out_specs=tuple(blocks),
        compiler_params=pltpu.CompilerParams(vmem_limit_bytes=60 * 2**20),
    )(*results)


def solution(mesh):
    in_specs = (
        P("seq", "head"),
        P("seq", "head"),
        P("seq", "head"),
        P("seq", None),
        P("head", "seq", None),
        P("head", None),
    )
    out_specs = (P("seq", "head"), P("seq", "head"), P("seq", "head"), P("seq", "head"))
    run = functools.partial(body, mesh.shape["seq"], mesh.shape["head"])
    return jax.shard_map(run, mesh=mesh, in_specs=in_specs, out_specs=out_specs, check_vma=False)
```
